128 devices in a mesh: patch: 32 (over x, z, core), grp: 4 (over y).
Axes of the slice: x: 4, y: 4, z: 4, core: 2. Of those that a mesh axis runs over, the one named last changes fastest.
Arguments:
- incident: float32 [16, 262144], P(None, ('patch', 'grp')), may hold values from -6 to 6
- self_term: float32 [262144], P(('patch', 'grp')), may hold values from 1 to 3
- near_field: bfloat16 [262144, 2304], P(('patch', 'grp')), may hold values from -0.125 to 0.125
- history: bfloat16 [8, 16, 262144], P(None, None, 'patch'), may hold values from -6 to 6
- ret_values: bfloat16 [32768, 128, 128], P(('patch', 'grp')), may hold values from -0.125 to 0.125
- slot_row: int32 [32768], P(('patch', 'grp')), may hold values from 0 to 15
- slot_col: int32 [32768], P(('patch', 'grp')), may hold values from 0 to 191
- slot_delay: int32 [32768], P(('patch', 'grp')), may hold values from 0 to 7
- live_count: int32 [128], P(('patch', 'grp')), may hold values from 32 to 256, as said below
Outputs:
- current: float32 [16, 262144], P(None, ('patch', 'grp'))
- newest: bfloat16 [16, 262144], P(None, 'patch')
The draws below stay inside these ranges and needn't reach their ends.
Inputs may be any that keep to these rules, and one draw needn't show every extreme that they name: The first live_count[d] slots of shard d are live, the rest ignored; some shard has all 256 slots live.
All inputs are finite; a program needn't handle non-finite values.
Results may differ from the reference program's by a relative error of at most 0.0055.
Values may be sent and summed in bfloat16 or wider, within the bound.
No kernel may reach another device: no remote copies, remote signals or barrier semaphores. Data moves between devices by JAX's collectives and lax.ppermute only.
A program may use at most 128 MiB of HBM per device.

```python
import math
import jax
import jax.numpy as jnp
from jax import lax

BLK = 128
WAVES = 16
DELAYS = 8
SWEEPS = 4
RB = 16
SLOTS = 256
UNKNOWNS = 262144
N_PATCH = 32
N_GRP = 4
DEVICES = 128


def draw_live_count(key, part):
    lowest = max(1, SLOTS // 8)
    key_a = jax.random.fold_in(key, 11)
    key_b = jax.random.fold_in(key, 12)
    ranks = jax.random.randint(key_a, (DEVICES,), 0, 64)
    counts = lowest + (SLOTS - lowest) * (ranks * ranks) // 4096
    busiest = jax.random.randint(key_b, (), 0, DEVICES)
    return counts.at[busiest].set(SLOTS).astype(jnp.int32)


def touch_ends(entries, key, smallest, top_value):
    longest = entries.shape.index(max(entries.shape))
    spots = []
    for shift in (0, 1):
        where = [jax.random.randint(jax.random.fold_in(key, axis), (), 0, length) for axis, length in enumerate(entries.shape)]
        where[longest] = (where[longest] + shift) % entries.shape[longest]
        spots.append(tuple(where))
    return entries.at[spots[0]].set(smallest).at[spots[1]].set(top_value)


def shard_levels(own_key, extent, split, smallest, high):
    loudness, own = 1.0, jax.random.fold_in(own_key, 6)
    for dim, parts in split:
        steps = jnp.exp(jax.random.uniform(jax.random.fold_in(own, dim), (parts,), jnp.float32, smallest / len(split), high / len(split)))
        loudness = loudness * jnp.repeat(steps, extent[dim] // parts).reshape([-1 if axis == dim else 1 for axis in range(len(extent))])
    return loudness


def bell_draw(key, dims, scale, most, pieces=(), held_as=jnp.bfloat16):
    entries = jax.random.normal(key, dims, jnp.float32) * scale
    if len(pieces) > 0:
        entries = shard_levels(key, dims, pieces, -0.22, 0.18) * entries
    return jnp.clip(entries, min=-most, max=most).astype(held_as)


def setup_inputs(seed: int = 0) -> dict:
    key_list = jax.random.split(jax.random.key(seed), 10)
    return {
        "incident": bell_draw(key_list[0], (WAVES, UNKNOWNS), 1.0, 6.0, ((1, 128),), jnp.float32),
        "self_term": jnp.clip(jnp.exp(math.log(3.0) - 1.0986123 * jax.random.uniform(key_list[1], (UNKNOWNS,), jnp.float32) ** shard_levels(key_list[1], (UNKNOWNS,), ((0, 128),), -0.2, 0.2)), 1.0, 3.0),
        "near_field": bell_draw(key_list[2], (UNKNOWNS, (RB + 2) * BLK), ((RB + 2) * BLK) ** -0.5, 0.125, ((0, 128),)),
        "history": bell_draw(key_list[3], (DELAYS, WAVES, UNKNOWNS), 1.0, 6.0, ((2, 32),)),
        "ret_values": bell_draw(key_list[4], (DEVICES * SLOTS, BLK, BLK), (BLK * SLOTS // RB) ** -0.5, 0.125, ((0, 128),)),
        "slot_row": touch_ends(jax.random.randint(key_list[5], (DEVICES * SLOTS,), 0, RB), jax.random.fold_in(key_list[5], 1), 0, RB - 1).astype(jnp.int32),
        "slot_col": touch_ends(jax.random.randint(key_list[6], (DEVICES * SLOTS,), 0, 3 * RB * N_GRP), jax.random.fold_in(key_list[6], 1), 0, (3 * RB * N_GRP) - 1).astype(jnp.int32),
        "slot_delay": touch_ends(jax.random.randint(key_list[7], (DEVICES * SLOTS,), 0, DELAYS), jax.random.fold_in(key_list[7], 1), 0, DELAYS - 1).astype(jnp.int32),
        "live_count": draw_live_count(jax.random.fold_in(key_list[9], 71), 0),
    }


def reference(incident, self_term, near_field, history, ret_values, slot_row, slot_col, slot_delay, live_count):
    patch_unk = RB * BLK * N_GRP
    padded = jnp.pad(history, ((0, 0), (0, 0), (patch_unk, patch_unk)))
    values_all = ret_values.reshape(DEVICES, SLOTS, BLK, BLK)
    rows_all = slot_row.reshape(DEVICES, SLOTS)
    cols_all = slot_col.reshape(DEVICES, SLOTS)
    delays_all = slot_delay.reshape(DEVICES, SLOTS)

    def one_device(packed):
        device, values, rows, cols, delays, limit = packed
        patch_id = (device // N_GRP).astype(jnp.int32)
        window = lax.dynamic_slice_in_dim(padded, (patch_id * patch_unk).astype(jnp.int32), 3 * patch_unk, 2)
        window = window.reshape(DELAYS, WAVES, 3 * RB * N_GRP, BLK)
        blocks = window[delays, :, cols, :]
        prods = jnp.einsum("swj,sij->swi", blocks.astype(jnp.float32), values.astype(jnp.float32))
        alive = (jnp.arange(SLOTS, dtype=jnp.int32) < limit).astype(jnp.float32)
        onehot = (rows[None, :] == jnp.arange(RB, dtype=jnp.int32)[:, None]).astype(jnp.float32) * alive[None, :]
        summed = jnp.einsum("rs,swi->wri", onehot, prods, precision=lax.Precision.HIGHEST)
        return summed.reshape(WAVES, RB * BLK)

    retarded = lax.map(one_device, (jnp.arange(DEVICES, dtype=jnp.int32), values_all, rows_all, cols_all, delays_all, live_count))
    retarded = jnp.transpose(retarded, (1, 0, 2)).reshape(WAVES, RB * BLK * DEVICES)
    rhs = incident - retarded
    near_wide = near_field.astype(jnp.float32).reshape(N_PATCH, N_GRP, RB * BLK, (RB + 2) * BLK)
    sweep_in = history[0]
    current = sweep_in.astype(jnp.float32)
    for sweep in range(SWEEPS):
        spread = sweep_in.astype(jnp.float32).reshape(WAVES, N_PATCH, N_GRP, RB * BLK)
        left_edge = jnp.pad(spread[:, :-1, :, -BLK:], ((0, 0), (1, 0), (0, 0), (0, 0)))
        right_edge = jnp.pad(spread[:, 1:, :, :BLK], ((0, 0), (0, 1), (0, 0), (0, 0)))
        extended = jnp.concatenate([left_edge, spread, right_edge], axis=3)
        coupling = jnp.einsum("wpgk,pgik->wpgi", extended, near_wide).reshape(WAVES, RB * BLK * DEVICES)
        current = (rhs - coupling) / self_term[None, :]
        sweep_in = current.astype(jnp.bfloat16)
    return current, sweep_in
```

```python
import jax
import jax.numpy as jnp
from jax import lax
from jax.experimental import pallas as pl
from jax.experimental.pallas import tpu as pltpu
from jax.sharding import PartitionSpec as P

BLK = 128
WAVES = 16
DELAYS = 8
SWEEPS = 4
RB = 16
SLOTS = 256
OWN = RB * BLK
EDGE = OWN + BLK
PATCH = 4 * OWN
COLS = PATCH // BLK
UNROLL = 8
ROWS = 256
NT = (((1,), (1,)), ((), ()))

VMEM = pl.BlockSpec(memory_space=pltpu.VMEM)
SMEM = pl.BlockSpec(memory_space=pltpu.SMEM)


def f32(*shape):
    return jax.ShapeDtypeStruct(shape, jnp.float32)


def bf16(*shape):
    return jax.ShapeDtypeStruct(shape, jnp.bfloat16)


def in_vmem(x):
    return pltpu.with_memory_space_constraint(x, pltpu.VMEM)


def call(body, out, ins, outs, args, flops, touched, scratch=()):
    return pl.pallas_call(
        body,
        out_shape=out,
        in_specs=ins,
        out_specs=outs,
        scratch_shapes=scratch,
        compiler_params=pltpu.CompilerParams(vmem_limit_bytes=30 * 2**20),
        cost_estimate=pl.CostEstimate(flops=flops, bytes_accessed=touched, transcendentals=0),
    )(*args)


def add_slots(count, codes, values, acc, block_of):
    def step(i, carry):
        found = []
        for j in range(0, UNROLL, 2):
            pair = []
            for k in (j, j + 1):
                at = i * UNROLL + k
                code = codes[at]
                block = block_of(code)
                block = jnp.where(at < count, block, jnp.zeros_like(block))
                pair.append((code, block))
            (code_a, a), (code_b, b) = pair
            zero = jnp.zeros_like(a)
            left = jnp.concatenate(
                [jnp.concatenate([a, zero], axis=1), jnp.concatenate([zero, b], axis=1)], axis=0
            )
            right = jnp.concatenate([values[code_a & 255], values[code_b & 255]], axis=1)
            both = lax.dot_general(left, right, NT, preferred_element_type=jnp.float32)
            found.append((code_a, both[:WAVES]))
            found.append((code_b, both[WAVES:]))
        for code, part in found:
            row = (code >> 8) & 15
            acc[row] = acc[row] + part
        return carry

    lax.fori_loop(0, (count + UNROLL - 1) // UNROLL, step, 0)


def own_coupling(x, near, out):
    def step(i, carry):
        at = pl.multiple_of(i * ROWS, ROWS)
        rows = near[pl.ds(at, ROWS), BLK:EDGE]
        out[:, pl.ds(at, ROWS)] = lax.dot_general(x, rows, NT, preferred_element_type=jnp.float32)
        return carry

    lax.fori_loop(0, OWN // ROWS, step, 0)


def edge_coupling(parity, cross, near_side, near):
    left = jnp.where(parity == 0, cross, near_side)
    right = jnp.where(parity == 0, near_side, cross)
    both = jnp.concatenate([left, right], axis=1)
    out = []
    for at in range(0, OWN, ROWS):
        rows = jnp.concatenate(
            [near[at : at + ROWS, :BLK], near[at : at + ROWS, EDGE:]], axis=1
        )
        out.append(lax.dot_general(both, rows, NT, preferred_element_type=jnp.float32))
    return out


def first_body(
    who, live, slot_row, slot_col, slot_delay, values, near, own, side,
    acc, coupling, codes_out, codes,
):
    parity, group = who[0], who[1]
    limit = live[0]

    def sort(s, counts):
        home, far = counts
        col = slot_col[s]
        third = jnp.where(col >= 2 * COLS, 2, jnp.where(col >= COLS, 1, 0))
        is_far = third == jnp.where(parity == 0, 0, 2)
        code = (
            s
            | (slot_row[s] << 8)
            | (slot_delay[s] << 12)
            | ((col - third * COLS) << 15)
            | (jnp.where(third == 1, 0, 1) << 21)
        )
        codes[home] = code
        codes_out[1 + far] = code
        alive = s < limit
        home = home + jnp.where(alive & jnp.logical_not(is_far), 1, 0)
        far = far + jnp.where(alive & is_far, 1, 0)
        return home, far

    home, far = lax.fori_loop(0, SLOTS, sort, (0, 0))
    for k in range(UNROLL):
        codes[home + k] = 0
        codes_out[1 + far + k] = 0
    codes_out[0] = far
    acc[...] = jnp.zeros_like(acc)

    def block_of(code):
        delay = (code >> 12) & 7
        at = pl.multiple_of(((code >> 15) & 63) * BLK, BLK)
        return jnp.where(
            ((code >> 21) & 1) == 1,
            side[delay, :, pl.ds(at, BLK)],
            own[delay, :, pl.ds(at, BLK)],
        )

    add_slots(home, codes, values, acc, block_of)
    start = pl.multiple_of(group * OWN, OWN)
    own_coupling(own[0, :, pl.ds(start, OWN)], near, coupling)


def finish(rhs, coupling, parts, self_term):
    out = []
    for i, part in enumerate(parts):
        at = slice(i * ROWS, (i + 1) * ROWS)
        out.append((rhs[:, at] - (coupling[:, at] + part)) / self_term[:, at])
    return jnp.concatenate(out, axis=1)


def give_edges(parity, x, to_cross, to_side):
    first, last = x[:, :BLK], x[:, OWN - BLK :]
    to_cross[...] = jnp.where(parity == 0, first, last)
    to_side[...] = jnp.where(parity == 0, last, first)


def second_body(
    who, codes, values, near, cross, side, acc, coupling, incident, self_term,
    rhs, x_out, to_cross, to_side, total,
):
    parity, group = who[0], who[1]
    total[...] = acc[...]

    def block_of(code):
        delay = (code >> 12) & 7
        at = pl.multiple_of(((code >> 15) & 63) * BLK, BLK)
        return cross[delay, :, pl.ds(at, BLK)]

    add_slots(codes[0], _Shifted(codes), values, total, block_of)
    for r in range(RB):
        at = slice(r * BLK, (r + 1) * BLK)
        rhs[:, at] = incident[:, at] - total[r]
    first = pl.multiple_of(group * OWN, BLK)
    last = pl.multiple_of(group * OWN + OWN - BLK, BLK)
    cross_at = pl.multiple_of(jnp.where(parity == 0, last, first), BLK)
    side_at = pl.multiple_of(jnp.where(parity == 0, first, last), BLK)
    parts = edge_coupling(
        parity, cross[0, :, pl.ds(cross_at, BLK)], side[0, :, pl.ds(side_at, BLK)], near
    )
    x = finish(rhs, coupling, parts, self_term).astype(jnp.bfloat16)
    x_out[...] = x
    give_edges(parity, x, to_cross, to_side)


class _Shifted:
    def __init__(self, ref):
        self.ref = ref

    def __getitem__(self, at):
        return self.ref[at + 1]


def own_body(x, near, out):
    own_coupling(x[...], near, out)


def sweep_body(who, near, cross, side, coupling, rhs, self_term, x_out, to_cross, to_side):
    parity = who[0]
    parts = edge_coupling(parity, cross[...], side[...], near)
    x = finish(rhs, coupling, parts, self_term).astype(jnp.bfloat16)
    x_out[...] = x
    give_edges(parity, x, to_cross, to_side)


def last_body(who, near, cross, side, coupling, rhs, self_term, current, x_out):
    parts = edge_coupling(who[0], cross[...], side[...], near)
    x = finish(rhs, coupling, parts, self_term)
    current[...] = x
    x_out[...] = x.astype(jnp.bfloat16)


def join_body(who, x, after, opposite, before, out):
    group = who[1]
    for shift, part in enumerate((x, after, opposite, before)):
        owner = (group + shift) % 4
        out[:, pl.ds(pl.multiple_of(owner * OWN, OWN), OWN)] = part[...]


def body(
    incident, self_term, near_field, history, ret_values, slot_row, slot_col, slot_delay, live_count
):
    count = lax.axis_size("patch")
    patch, group = lax.axis_index("patch"), lax.axis_index("grp")
    who = jnp.stack([patch % 2, group]).astype(jnp.int32)
    diag = self_term[None, :]
    chip = [(i, i ^ 1) for i in range(count)]
    links = [(i, i + 1) for i in range(1, count - 1, 2)]
    links = links + [(b, a) for a, b in links]

    cross = lax.ppermute(history, "patch", links)
    side = lax.ppermute(history, "patch", chip)
    values, near = in_vmem(ret_values), in_vmem(near_field)

    acc, coupling, codes = call(
        first_body,
        (f32(RB, WAVES, BLK), f32(WAVES, OWN), jax.ShapeDtypeStruct((SLOTS + 2 * UNROLL,), jnp.int32)),
        [SMEM] * 5 + [VMEM] * 4,
        (VMEM, VMEM, SMEM),
        (who, live_count, slot_row, slot_col, slot_delay, values, near, history, side),
        2 * 10**9,
        20 * 10**6,
        [pltpu.SMEM((SLOTS + 2 * UNROLL,), jnp.int32)],
    )
    rhs, x, to_cross, to_side = call(
        second_body,
        (f32(WAVES, OWN), bf16(WAVES, OWN), bf16(WAVES, BLK), bf16(WAVES, BLK)),
        [SMEM] * 2 + [VMEM] * 8,
        (VMEM,) * 4,
        (who, codes, values, near, cross, side, acc, coupling, incident, diag),
        10**9,
        10**6,
        [pltpu.VMEM((RB, WAVES, BLK), jnp.float32)],
    )
    for sweep in range(1, SWEEPS):
        edge_cross = lax.ppermute(to_cross, "patch", links)
        edge_side = lax.ppermute(to_side, "patch", chip)
        coupling = call(
            own_body, f32(WAVES, OWN), [VMEM] * 2, VMEM, (x, near), 2 * WAVES * OWN * OWN, 8 * 2**20
        )
        last = sweep == SWEEPS - 1
        made = call(
            last_body if last else sweep_body,
            (f32(WAVES, OWN), bf16(WAVES, OWN))
            if last
            else (bf16(WAVES, OWN), bf16(WAVES, BLK), bf16(WAVES, BLK)),
            [SMEM] + [VMEM] * 6,
            (VMEM,) * (2 if last else 3),
            (who, near, edge_cross, edge_side, coupling, rhs, diag),
            2 * WAVES * OWN * 2 * BLK,
            2**20,
        )
        if last:
            current, x = made
        else:
            x, to_cross, to_side = made
    turns = [
        lax.ppermute(x, "grp", [((i + shift) % 4, i) for i in range(4)]) for shift in (1, 2, 3)
    ]
    newest = call(
        join_body, bf16(WAVES, PATCH), [SMEM] + [VMEM] * 4, VMEM, (who, x, *turns), 0, 2**20
    )
    return current, newest


def solution(mesh):
    placed = (
        P(None, ("patch", "grp")),
        P(("patch", "grp")),
        P(("patch", "grp"), None),
        P(None, None, "patch"),
        P(("patch", "grp"), None, None),
        P(("patch", "grp")),
        P(("patch", "grp")),
        P(("patch", "grp")),
        P(("patch", "grp")),
    )
    return jax.shard_map(
        body,
        mesh=mesh,
        in_specs=placed,
        out_specs=(P(None, ("patch", "grp")), P(None, "patch")),
        check_vma=False,
    )
```

```python
import jax
import jax.numpy as jnp
from jax import lax
from jax.experimental import pallas as pl
from jax.experimental.pallas import tpu as pltpu
from jax.sharding import PartitionSpec as P

BLK = 128
WAVES = 16
DELAYS = 8
SWEEPS = 4
RB = 16
SLOTS = 256
OWN = RB * BLK
EDGE = OWN + BLK
PATCH = 4 * OWN
COLS = PATCH // BLK
UNROLL = 32
ROWS = 256
NT = (((1,), (1,)), ((), ()))

VMEM = pl.BlockSpec(memory_space=pltpu.VMEM)
HBM = pl.BlockSpec(memory_space=pl.ANY)
SMEM = pl.BlockSpec(memory_space=pltpu.SMEM)


def f32(*shape):
    return jax.ShapeDtypeStruct(shape, jnp.float32)


def bf16(*shape):
    return jax.ShapeDtypeStruct(shape, jnp.bfloat16)


def in_vmem(x):
    return pltpu.with_memory_space_constraint(x, pltpu.VMEM)


def in_hbm(x):
    return pltpu.with_memory_space_constraint(x, pltpu.HBM)


def call(body, out, ins, outs, args, flops, touched, scratch=()):
    return pl.pallas_call(
        body,
        out_shape=out,
        in_specs=ins,
        out_specs=outs,
        scratch_shapes=scratch,
        compiler_params=pltpu.CompilerParams(vmem_limit_bytes=16 * 2**20),
        cost_estimate=pl.CostEstimate(flops=flops, bytes_accessed=touched, transcendentals=0),
    )(*args)


def add_slots(count, codes, values, acc, block_of):
    def step(i, carry):
        found = []
        for j in range(0, UNROLL, 2):
            pair = []
            for k in (j, j + 1):
                at = i * UNROLL + k
                code = codes[at]
                block = block_of(code)
                block = jnp.where(at < count, block, jnp.zeros_like(block))
                pair.append((code, block))
            (code_a, a), (code_b, b) = pair
            zero = jnp.zeros_like(a)
            left = jnp.concatenate(
                [jnp.concatenate([a, zero], axis=1), jnp.concatenate([zero, b], axis=1)], axis=0
            )
            right = jnp.concatenate([values[code_a & 255], values[code_b & 255]], axis=1)
            both = lax.dot_general(left, right, NT, preferred_element_type=jnp.float32)
            found.append((code_a, both[:WAVES]))
            found.append((code_b, both[WAVES:]))
        for code, part in found:
            row = (code >> 8) & 15
            acc[row] = acc[row] + part
        return carry

    lax.fori_loop(0, (count + UNROLL - 1) // UNROLL, step, 0)


def own_coupling(x, near, out):
    for at in range(0, OWN, ROWS):
        rows = near[at : at + ROWS, BLK:EDGE]
        out[:, at : at + ROWS] = lax.dot_general(x, rows, NT, preferred_element_type=jnp.float32)


def edge_coupling(parity, cross, near_side, near):
    left = jnp.where(parity == 0, cross, near_side)
    right = jnp.where(parity == 0, near_side, cross)
    both = jnp.concatenate([left, right], axis=1)
    out = []
    for at in range(0, OWN, ROWS):
        rows = jnp.concatenate(
            [near[at : at + ROWS, :BLK], near[at : at + ROWS, EDGE:]], axis=1
        )
        out.append(lax.dot_general(both, rows, NT, preferred_element_type=jnp.float32))
    return out


def home_body(codes, values, own, side, acc):
    acc[...] = jnp.zeros_like(acc)

    def block_of(code):
        delay = (code >> 12) & 7
        at = pl.multiple_of(((code >> 15) & 63) * BLK, BLK)
        return jnp.where(
            ((code >> 21) & 1) == 1,
            side[delay, :, pl.ds(at, BLK)],
            own[delay, :, pl.ds(at, BLK)],
        )

    add_slots(codes[0], _Shifted(codes), values, acc, block_of)


def sort_slots(span, parity, limit, counts, slot_row, slot_col, slot_delay, home_codes, far_codes):
    home, far = counts
    for s in span:
        col = slot_col[s]
        third = jnp.where(col >= 2 * COLS, 2, jnp.where(col >= COLS, 1, 0))
        is_far = third == 2 * parity
        code = (
            s
            | (slot_row[s] << 8)
            | (slot_delay[s] << 12)
            | ((col - third * COLS) << 15)
            | (jnp.where(third == 1, 0, 1) << 21)
        )
        home_codes[1 + home] = code
        far_codes[1 + far] = code
        alive = jnp.where(s < limit, 1, 0)
        passed = jnp.where(is_far, alive, 0)
        home, far = home + alive - passed, far + passed
    return home, far


def close_lists(counts, home_codes, far_codes):
    home, far = counts
    home_codes[0] = home
    far_codes[0] = far

    def clear(k, carry):
        home_codes[1 + home + k] = 0
        far_codes[1 + far + k] = 0
        return carry

    lax.fori_loop(0, UNROLL, clear, 0)


class _Shifted:
    def __init__(self, ref):
        self.ref = ref

    def __getitem__(self, at):
        return self.ref[at + 1]


def core_parity():
    return lax.rem(lax.axis_index("patch"), 2)


def lanes(at):
    return pl.ds(pl.multiple_of(at, BLK), BLK)


def places():
    parity = core_parity()
    return {
        "cross_cols": lanes(parity * EDGE),
        "side_cols": lanes((1 - parity) * EDGE),
        "outer": lanes(parity * (OWN - BLK)),
        "inner": lanes((1 - parity) * (OWN - BLK)),
    }


def chunks():
    return [slice(at, at + ROWS) for at in range(0, OWN, ROWS)]


def spans():
    return [pl.ds(at, ROWS) for at in range(0, OWN, ROWS)]


def nt(a, b):
    return lax.dot_general(a, b, NT, preferred_element_type=jnp.float32)


def nn(a, b):
    return jnp.dot(a, b, preferred_element_type=jnp.float32)


def response_1_body(
    live, row_hbm, col_hbm, delay_hbm, self_hbm, near_hbm, history,
    near, coupling, first, second, inner, inv, home_codes, far_codes,
    edge, newest, slot_row, slot_col, slot_delay, sems,
):
    parity, group = core_parity(), lax.axis_index("grp")
    at = places()
    start = pl.multiple_of(group * OWN, OWN)
    pairs = [
        (near_hbm.at[:, at["cross_cols"]], edge),
        (self_hbm, inv),
        (history.at[0, :, pl.ds(start, OWN)], newest),
        (row_hbm, slot_row),
        (col_hbm, slot_col),
        (delay_hbm, slot_delay),
    ] + [(near_hbm.at[rows], near.at[rows]) for rows in spans()]
    copies = [pltpu.make_async_copy(a, b, sems.at[i]) for i, (a, b) in enumerate(pairs)]
    for copy in copies:
        copy.start()
    eye = jnp.where(
        lax.broadcasted_iota(jnp.int32, (BLK, BLK), 0) == lax.broadcasted_iota(jnp.int32, (BLK, BLK), 1), 1.0, 0.0
    ).astype(jnp.bfloat16)
    copies[1].wait()
    inv[...] = 1.0 / inv[...]
    copies[0].wait()
    for rows in chunks():
        first[:, rows] = (-nt(eye, edge[rows]) * inv[:, rows]).astype(jnp.bfloat16)
    for copy in copies[2:6]:
        copy.wait()
    inner[...] = first[:, at["inner"]]
    limit = live[0]
    counts = (jnp.int32(0), jnp.int32(0))
    both = jnp.concatenate([first[...], newest[...]], axis=0)
    share = SLOTS // len(chunks())
    for i, (rows, copy) in enumerate(zip(chunks(), copies[6:])):
        copy.wait()
        counts = sort_slots(
            range(i * share, (i + 1) * share), parity, limit, counts,
            slot_row, slot_col, slot_delay, home_codes, far_codes,
        )
        made = nt(both, near[rows, BLK:EDGE])
        second[:, rows] = (-made[:BLK] * inv[:, rows]).astype(jnp.bfloat16)
        coupling[:, rows] = made[BLK:]
    close_lists(counts, home_codes, far_codes)


def response_2_body(near, inv, first, second, side, both, inner, corners):
    at = places()
    both[:BLK] = second[...]
    for rows in chunks():
        both[BLK:, rows] = (-nt(side[...], near[rows, at["side_cols"]]) * inv[:, rows]).astype(jnp.bfloat16)
    inner[...] = both[:, at["inner"]]
    corners[:BLK] = first[:, at["outer"]]
    corners[BLK:] = both[:, at["outer"]]


def response_3_body(near, inv, both, side, third):
    at = places()
    turned = jnp.concatenate([side[BLK:], side[:BLK]], axis=0)
    for rows in chunks():
        made = nt(both[...], near[rows, BLK:EDGE]) + nt(turned, near[rows, at["side_cols"]])
        third[:, rows] = (-made * inv[:, rows]).astype(jnp.bfloat16)


def second_body(
    codes, values, near, cross, side, acc, coupling, incident, inv, after,
    rhs, x_out, inner, total,
):
    parity, group = core_parity(), lax.axis_index("grp")
    total[...] = acc[...]

    def block_of(code):
        delay = (code >> 12) & 7
        at = pl.multiple_of(((code >> 15) & 63) * BLK, BLK)
        return cross[delay, :, pl.ds(at, BLK)]

    add_slots(codes[0], _Shifted(codes), values, total, block_of)
    for r in range(RB):
        at = slice(r * BLK, (r + 1) * BLK)
        rhs[:, at] = incident[:, at] - total[r]
    first = group * OWN
    last = group * OWN + OWN - BLK
    from_cross = cross[0, :, lanes(jnp.where(parity == 0, last, first))]
    from_side = side[0, :, lanes(jnp.where(parity == 0, first, last))]
    parts = edge_coupling(parity, from_cross, from_side, near)
    for rows, part in zip(chunks(), parts):
        x_out[:, rows] = ((rhs[:, rows] - (coupling[:, rows] + part)) * inv[:, rows]).astype(jnp.bfloat16)
    inner[...] = x_out[:, places()["inner"]]


def own_body(x, near, out):
    own_coupling(x[...], near, out)


def side_body(near, side, coupling, rhs, inv, y_out, inner):
    at = places()
    for rows in chunks():
        part = coupling[:, rows] + nt(side[...], near[rows, at["side_cols"]])
        y_out[:, rows] = ((rhs[:, rows] - part) * inv[:, rows]).astype(jnp.bfloat16)
    inner[...] = y_out[:, at["inner"]]


def early_body(near, x, y, side, rhs, inv, corners, near_by, far):
    at = places()
    rows = pl.ds(pl.multiple_of(core_parity() * (OWN - BLK), BLK), BLK)
    part = nt(y[...], near[rows, BLK:EDGE]) + nt(side[...], near[rows, at["side_cols"]])
    third = (rhs[:, at["outer"]] - part) * inv[:, at["outer"]]
    near_by[:WAVES] = x[:, at["outer"]]
    near_by[WAVES : 2 * WAVES] = y[:, at["outer"]]
    near_by[2 * WAVES : 3 * WAVES] = third.astype(jnp.bfloat16)
    near_by[3 * WAVES :] = corners[...]
    far[...] = x[:, at["outer"]]


def whole_body(near, x, side, rhs, inv, y_out, inner):
    at = places()
    for rows in chunks():
        part = nt(x[...], near[rows, BLK:EDGE]) + nt(side[...], near[rows, at["side_cols"]])
        y_out[:, rows] = ((rhs[:, rows] - part) * inv[:, rows]).astype(jnp.bfloat16)
    inner[...] = y_out[:, at["inner"]]


def edges_body(near_by, far, first, x, y, shared, third):
    at = places()
    one, mine = near_by[:WAVES], x[:, at["outer"]]
    mine_2 = y[:, at["outer"]].astype(jnp.float32) + nn(one, first[:, at["outer"]])
    corners = near_by[3 * WAVES :]
    two = near_by[WAVES : 2 * WAVES].astype(jnp.float32) + nn(mine, corners[:BLK])
    three = near_by[2 * WAVES : 3 * WAVES].astype(jnp.float32) + nn(mine, corners[BLK : 2 * BLK])
    three = three + nn(far[...], corners[2 * BLK :]) + nn(mine_2.astype(jnp.bfloat16), corners[:BLK])
    shared[:WAVES] = one
    shared[WAVES:] = two.astype(jnp.bfloat16)
    third[...] = three.astype(jnp.bfloat16)


def last_body(
    near, side, coupling, rhs, inv, mine, mine_3, other, first, both, third, current, x_out
):
    at = places()
    one = jnp.concatenate([mine[:WAVES], other[:WAVES]], axis=1)
    two = jnp.concatenate([mine[WAVES:], other[WAVES:]], axis=1)
    for rows in chunks():
        part = coupling[:, rows] + nt(side[...], near[rows, at["side_cols"]])
        y = (rhs[:, rows] - part) * inv[:, rows]
        x = y + (nn(one, third[:, rows]) + nn(two, both[:, rows]) + nn(mine_3[...], first[:, rows]))
        current[:, rows] = x
        x_out[:, rows] = x.astype(jnp.bfloat16)


def join_body(x, one, two, three, out):
    group = lax.axis_index("grp")
    for k, part in enumerate((x, one, two, three)):
        owner = group ^ k
        out[:, pl.ds(pl.multiple_of(owner * OWN, OWN), OWN)] = part[...]


def body(
    incident, self_term, near_field, history, ret_values, slot_row, slot_col, slot_delay, live_count
):
    count = lax.axis_size("patch")
    inv = self_term[None, :]
    chip = [(i, i ^ 1) for i in range(count)]
    links = [(i, i + 1) for i in range(1, count - 1, 2)]
    links = links + [(b, a) for a, b in links]
    beyond = [(i, i + 3) for i in range(1, count - 3, 2)]
    beyond = beyond + [(b, a) for a, b in beyond]
    product = 2 * OWN * OWN

    cross = lax.ppermute(history, "patch", links)
    side = lax.ppermute(history, "patch", chip)
    values = in_vmem(ret_values)
    codes = pltpu.SMEM((SLOTS + 2 * UNROLL,), jnp.int32)

    near, coupling, first, second, inner, inv, home_codes, far_codes = call(
        response_1_body,
        (pltpu.VMEM((OWN, EDGE + BLK), jnp.bfloat16), f32(WAVES, OWN), bf16(BLK, OWN), bf16(BLK, OWN),
         bf16(BLK, BLK), f32(1, OWN), codes, codes),
        [SMEM] + [HBM] * 6,
        (VMEM,) * 6 + (SMEM,) * 2,
        (live_count,) + tuple(in_hbm(x) for x in (slot_row, slot_col, slot_delay, inv, near_field, history)),
        product * 144,
        8 * 2**20,
        [
            pltpu.VMEM((OWN, BLK), jnp.bfloat16),
            pltpu.VMEM((WAVES, OWN), jnp.bfloat16),
            pltpu.SMEM((SLOTS,), jnp.int32),
            pltpu.SMEM((SLOTS,), jnp.int32),
            pltpu.SMEM((SLOTS,), jnp.int32),
            pltpu.SemaphoreType.DMA((6 + OWN // ROWS,)),
        ],
    )
    near = in_vmem(near)
    home_codes, far_codes = (pltpu.with_memory_space_constraint(x, pltpu.SMEM) for x in (home_codes, far_codes))
    both, inner, corners = call(
        response_2_body,
        (bf16(2 * BLK, OWN), bf16(2 * BLK, BLK), bf16(3 * BLK, BLK)),
        [VMEM] * 5,
        (VMEM,) * 3,
        (near, inv, first, second, lax.ppermute(inner, "patch", chip)),
        product * 16,
        2**20,
    )
    third = call(
        response_3_body,
        bf16(2 * BLK, OWN),
        [VMEM] * 4,
        VMEM,
        (near, inv, both, lax.ppermute(inner, "patch", chip)),
        product * 256,
        8 * 2**20,
    )
    acc = call(
        home_body,
        f32(RB, WAVES, BLK),
        [SMEM] + [VMEM] * 3,
        VMEM,
        (home_codes, values, in_vmem(history), in_vmem(side)),
        2 * 10**9,
        10 * 10**6,
    )
    rhs, x, inner = call(
        second_body,
        (f32(WAVES, OWN), bf16(WAVES, OWN), bf16(WAVES, BLK)),
        [SMEM] + [VMEM] * 8 + [HBM],
        (VMEM,) * 3,
        (far_codes, values, near, in_vmem(cross), in_vmem(side), acc, coupling, incident, inv, third),
        10**9,
        10**6,
        [pltpu.VMEM((RB, WAVES, BLK), jnp.float32)],
    )
    edge = lax.ppermute(inner, "patch", chip)
    coupling = call(own_body, f32(WAVES, OWN), [VMEM] * 2, VMEM, (x, near), product * 16, 8 * 2**20)
    y, inner = call(
        side_body,
        (bf16(WAVES, OWN), bf16(WAVES, BLK)),
        [VMEM] * 5,
        (VMEM,) * 2,
        (near, edge, coupling, rhs, inv),
        product,
        2**19,
    )
    edge = lax.ppermute(inner, "patch", chip)
    near_by, far = call(
        early_body,
        (bf16(3 * WAVES + 3 * BLK, BLK), bf16(WAVES, BLK)),
        [VMEM] * 7,
        (VMEM,) * 2,
        (near, x, y, edge, rhs, inv, corners),
        product,
        2**19,
    )
    near_by = lax.ppermute(near_by, "patch", links)
    far = lax.ppermute(far, "patch", beyond)
    y_3, inner = call(
        whole_body,
        (bf16(WAVES, OWN), bf16(WAVES, BLK)),
        [VMEM] * 5,
        (VMEM,) * 2,
        (near, y, edge, rhs, inv),
        product * 16,
        8 * 2**20,
    )
    edge = lax.ppermute(inner, "patch", chip)
    coupling = call(
        own_body, f32(WAVES, OWN), [VMEM] * 2, VMEM, (y_3, near), product * 16, 8 * 2**20
    )
    shared, mine_3 = call(
        edges_body,
        (bf16(2 * WAVES, BLK), bf16(WAVES, BLK)),
        [VMEM] * 5,
        (VMEM,) * 2,
        (near_by, far, first, x, y),
        product // 100,
        2**17,
    )
    other = lax.ppermute(shared, "patch", chip)
    current, x = call(
        last_body,
        (f32(WAVES, OWN), bf16(WAVES, OWN)),
        [VMEM] * 11,
        (VMEM,) * 2,
        (near, edge, coupling, rhs, inv, shared, mine_3, other, first, both, third),
        product * 4,
        2**21,
    )
    turns = [
        lax.ppermute(x, "grp", [(i, i ^ k) for i in range(4)]) for k in (1, 2, 3)
    ]
    newest = call(
        join_body, bf16(WAVES, PATCH), [VMEM] * 4, VMEM, (x, *turns), 0, 2**20
    )
    return current, newest


def solution(mesh):
    placed = (
        P(None, ("patch", "grp")),
        P(("patch", "grp")),
        P(("patch", "grp"), None),
        P(None, None, "patch"),
        P(("patch", "grp"), None, None),
        P(("patch", "grp")),
        P(("patch", "grp")),
        P(("patch", "grp")),
        P(("patch", "grp")),
    )
    return jax.shard_map(
        body,
        mesh=mesh,
        in_specs=placed,
        out_specs=(P(None, ("patch", "grp")), P(None, "patch")),
        check_vma=False,
    )
```

```python
import jax
import jax.numpy as jnp
from jax import lax
from jax.experimental import pallas as pl
from jax.experimental.pallas import tpu as pltpu
from jax.sharding import PartitionSpec as P

BLK = 128
WAVES = 16
DELAYS = 8
SWEEPS = 4
RB = 16
SLOTS = 256
OWN = RB * BLK
EDGE = OWN + BLK
PATCH = 4 * OWN
COLS = PATCH // BLK
HALF = OWN // 2
UNROLL = 32
ROWS = 256
NT = (((1,), (1,)), ((), ()))

VMEM = pl.BlockSpec(memory_space=pltpu.VMEM)
HBM = pl.BlockSpec(memory_space=pl.ANY)
SMEM = pl.BlockSpec(memory_space=pltpu.SMEM)


def f32(*shape):
    return jax.ShapeDtypeStruct(shape, jnp.float32)


def bf16(*shape):
    return jax.ShapeDtypeStruct(shape, jnp.bfloat16)


def in_vmem(x):
    return pltpu.with_memory_space_constraint(x, pltpu.VMEM)


def in_hbm(x):
    return pltpu.with_memory_space_constraint(x, pltpu.HBM)


def call(body, out, ins, outs, args, flops, touched, scratch=()):
    return pl.pallas_call(
        body,
        out_shape=out,
        in_specs=ins,
        out_specs=outs,
        scratch_shapes=scratch,
        compiler_params=pltpu.CompilerParams(vmem_limit_bytes=16 * 2**20),
        cost_estimate=pl.CostEstimate(flops=flops, bytes_accessed=touched, transcendentals=0),
    )(*args)


def add_slots(count, codes, values, acc, block_of):
    def step(i, carry):
        found = []
        for j in range(0, UNROLL, 2):
            pair = []
            for k in (j, j + 1):
                at = i * UNROLL + k
                code = codes[at]
                block = block_of(code)
                block = jnp.where(at < count, block, jnp.zeros_like(block))
                pair.append((code, block))
            (code_a, a), (code_b, b) = pair
            zero = jnp.zeros_like(a)
            left = jnp.concatenate(
                [jnp.concatenate([a, zero], axis=1), jnp.concatenate([zero, b], axis=1)], axis=0
            )
            right = jnp.concatenate([values[code_a & 255], values[code_b & 255]], axis=1)
            both = lax.dot_general(left, right, NT, preferred_element_type=jnp.float32)
            found.append((code_a, both[:WAVES]))
            found.append((code_b, both[WAVES:]))
        for code, part in found:
            row = (code >> 8) & 15
            acc[row] = acc[row] + part
        return carry

    lax.fori_loop(0, (count + UNROLL - 1) // UNROLL, step, 0)


def own_coupling(x, near, out):
    for at in range(0, OWN, ROWS):
        rows = near[at : at + ROWS, BLK:EDGE]
        out[:, at : at + ROWS] = lax.dot_general(x, rows, NT, preferred_element_type=jnp.float32)


def edge_coupling(parity, cross, near_side, near):
    left = jnp.where(parity == 0, cross, near_side)
    right = jnp.where(parity == 0, near_side, cross)
    both = jnp.concatenate([left, right], axis=1)
    out = []
    for at in range(0, OWN, ROWS):
        rows = jnp.concatenate(
            [near[at : at + ROWS, :BLK], near[at : at + ROWS, EDGE:]], axis=1
        )
        out.append(lax.dot_general(both, rows, NT, preferred_element_type=jnp.float32))
    return out


def home_body(codes, values, own, side, acc):
    acc[...] = jnp.zeros_like(acc)

    def block_of(code):
        delay = (code >> 12) & 7
        at = pl.multiple_of(((code >> 15) & 63) * BLK, BLK)
        return jnp.where(
            ((code >> 21) & 1) == 1,
            side[delay, :, pl.ds(at, BLK)],
            own[delay, :, pl.ds(at, BLK)],
        )

    add_slots(codes[0], _Shifted(codes), values, acc, block_of)


def sort_slots(span, parity, limit, counts, slot_row, slot_col, slot_delay, home_codes, far_codes):
    home, far = counts
    for s in span:
        col = slot_col[s]
        third = jnp.where(col >= 2 * COLS, 2, jnp.where(col >= COLS, 1, 0))
        is_far = third == 2 * parity
        code = (
            s
            | (slot_row[s] << 8)
            | (slot_delay[s] << 12)
            | ((col - third * COLS) << 15)
            | (jnp.where(third == 1, 0, 1) << 21)
        )
        home_codes[1 + home] = code
        far_codes[1 + far] = code
        alive = jnp.where(s < limit, 1, 0)
        passed = jnp.where(is_far, alive, 0)
        home, far = home + alive - passed, far + passed
    return home, far


def close_lists(counts, home_codes, far_codes):
    home, far = counts
    home_codes[0] = home
    far_codes[0] = far

    def clear(k, carry):
        home_codes[1 + home + k] = 0
        far_codes[1 + far + k] = 0
        return carry

    lax.fori_loop(0, UNROLL, clear, 0)


class _Shifted:
    def __init__(self, ref):
        self.ref = ref

    def __getitem__(self, at):
        return self.ref[at + 1]


def core_parity():
    return lax.rem(lax.axis_index("patch"), 2)


def lanes(at):
    return pl.ds(pl.multiple_of(at, BLK), BLK)


def places():
    parity = core_parity()
    return {
        "cross_cols": lanes(parity * EDGE),
        "side_cols": lanes((1 - parity) * EDGE),
        "outer": lanes(parity * (OWN - BLK)),
        "inner": lanes((1 - parity) * (OWN - BLK)),
    }


def chunks():
    return [slice(at, at + ROWS) for at in range(0, OWN, ROWS)]


def spans():
    return [pl.ds(at, ROWS) for at in range(0, OWN, ROWS)]


def nt(a, b):
    return lax.dot_general(a, b, NT, preferred_element_type=jnp.float32)


def nn(a, b):
    return jnp.dot(a, b, preferred_element_type=jnp.float32)


def response_1_body(
    live, row_hbm, col_hbm, delay_hbm, self_hbm, near_hbm, history,
    near, coupling, first, second, inner, inv, home_codes, far_codes,
    edge, newest, slot_row, slot_col, slot_delay, sems,
):
    parity, group = core_parity(), lax.axis_index("grp")
    at = places()
    start = pl.multiple_of(group * OWN, OWN)
    pairs = [
        (near_hbm.at[:, at["cross_cols"]], edge),
        (self_hbm, inv),
        (history.at[0, :, pl.ds(start, OWN)], newest),
        (row_hbm, slot_row),
        (col_hbm, slot_col),
        (delay_hbm, slot_delay),
    ] + [(near_hbm.at[rows], near.at[rows]) for rows in spans()]
    copies = [pltpu.make_async_copy(a, b, sems.at[i]) for i, (a, b) in enumerate(pairs)]
    for copy in copies:
        copy.start()
    eye = jnp.where(
        lax.broadcasted_iota(jnp.int32, (BLK, BLK), 0) == lax.broadcasted_iota(jnp.int32, (BLK, BLK), 1), 1.0, 0.0
    ).astype(jnp.bfloat16)
    copies[1].wait()
    inv[...] = 1.0 / inv[...]
    copies[0].wait()
    for rows in chunks():
        first[:, rows] = (-nt(eye, edge[rows]) * inv[:, rows]).astype(jnp.bfloat16)
    for copy in copies[2:6]:
        copy.wait()
    inner[...] = first[:, at["inner"]]
    limit = live[0]
    counts = (jnp.int32(0), jnp.int32(0))
    both = jnp.concatenate([first[...], newest[...]], axis=0)
    share = SLOTS // len(chunks())
    for i, (rows, copy) in enumerate(zip(chunks(), copies[6:])):
        copy.wait()
        counts = sort_slots(
            range(i * share, (i + 1) * share), parity, limit, counts,
            slot_row, slot_col, slot_delay, home_codes, far_codes,
        )
        made = nt(both, near[rows, BLK:EDGE])
        second[:, rows] = (-made[:BLK] * inv[:, rows]).astype(jnp.bfloat16)
        coupling[:, rows] = made[BLK:]
    close_lists(counts, home_codes, far_codes)


def response_2_body(near, inv, first, second, side, both, inner, corners):
    at = places()
    both[:BLK] = second[...]
    for rows in chunks():
        both[BLK:, rows] = (-nt(side[...], near[rows, at["side_cols"]]) * inv[:, rows]).astype(jnp.bfloat16)
    inner[...] = both[:, at["inner"]]
    corners[:BLK] = first[:, at["outer"]]
    corners[BLK:] = both[:, at["outer"]]


def response_3_body(near, inv, both, side, third):
    at = places()
    turned = jnp.concatenate([side[BLK:], side[:BLK]], axis=0)
    for rows in chunks():
        made = nt(both[...], near[rows, BLK:EDGE]) + nt(turned, near[rows, at["side_cols"]])
        third[:, rows] = (-made * inv[:, rows]).astype(jnp.bfloat16)


def second_body(
    codes, values, near, cross, side, acc, coupling, incident, inv, after,
    rhs, x_out, inner, total,
):
    parity, group = core_parity(), lax.axis_index("grp")
    total[...] = acc[...]

    def block_of(code):
        delay = (code >> 12) & 7
        at = pl.multiple_of(((code >> 15) & 63) * BLK, BLK)
        return cross[delay, :, pl.ds(at, BLK)]

    add_slots(codes[0], _Shifted(codes), values, total, block_of)
    for r in range(RB):
        at = slice(r * BLK, (r + 1) * BLK)
        rhs[:, at] = incident[:, at] - total[r]
    first = group * OWN
    last = group * OWN + OWN - BLK
    from_cross = cross[0, :, lanes(jnp.where(parity == 0, last, first))]
    from_side = side[0, :, lanes(jnp.where(parity == 0, first, last))]
    parts = edge_coupling(parity, from_cross, from_side, near)
    for rows, part in zip(chunks(), parts):
        x_out[:, rows] = ((rhs[:, rows] - (coupling[:, rows] + part)) * inv[:, rows]).astype(jnp.bfloat16)
    inner[...] = x_out[:, places()["inner"]]


def own_body(x, near, out):
    own_coupling(x[...], near, out)


def side_body(near, side, coupling, rhs, inv, x, y_out, far):
    at = places()
    for rows in chunks():
        part = coupling[:, rows] + nt(side[...], near[rows, at["side_cols"]])
        y_out[:, rows] = ((rhs[:, rows] - part) * inv[:, rows]).astype(jnp.bfloat16)
    far[...] = x[:, pl.ds(pl.multiple_of(core_parity() * HALF, HALF), HALF)]


def early_body(near, x, y, side, rhs, inv, near_by):
    at = places()
    rows = pl.ds(pl.multiple_of(core_parity() * (OWN - BLK), BLK), BLK)
    part = nt(y[...], near[rows, BLK:EDGE]) + nt(side[:, at["outer"]], near[rows, at["side_cols"]])
    third = (rhs[:, at["outer"]] - part) * inv[:, at["outer"]]
    near_by[:WAVES] = x[:, at["outer"]]
    near_by[WAVES : 2 * WAVES] = y[:, at["outer"]]
    near_by[2 * WAVES :] = third.astype(jnp.bfloat16)


def whole_body(near, x, side, rhs, inv, y_out, inner):
    at = places()
    for rows in chunks():
        part = nt(x[...], near[rows, BLK:EDGE]) + nt(side[:, at["outer"]], near[rows, at["side_cols"]])
        y_out[:, rows] = ((rhs[:, rows] - part) * inv[:, rows]).astype(jnp.bfloat16)
    inner[...] = y_out[:, at["inner"]]


def edges_body(near_by, far, corners, first, x, y, shared, third):
    at = places()
    one, mine = near_by[:WAVES], x[:, at["outer"]]
    mine_2 = y[:, at["outer"]].astype(jnp.float32) + nn(one, first[:, at["outer"]])
    two = near_by[WAVES : 2 * WAVES].astype(jnp.float32) + nn(mine, corners[:BLK])
    three = near_by[2 * WAVES :].astype(jnp.float32) + nn(mine, corners[BLK : 2 * BLK])
    three = three + nn(far[:, lanes((1 - core_parity()) * (HALF - BLK))], corners[2 * BLK :]) + nn(mine_2.astype(jnp.bfloat16), corners[:BLK])
    shared[:WAVES] = one
    shared[WAVES:] = two.astype(jnp.bfloat16)
    third[...] = three.astype(jnp.bfloat16)


def last_body(
    near, side, coupling, rhs, inv, mine, mine_3, other, first, both, third, current, x_out
):
    at = places()
    one = jnp.concatenate([mine[:WAVES], other[:WAVES]], axis=1)
    two = jnp.concatenate([mine[WAVES:], other[WAVES:]], axis=1)
    for rows in chunks():
        part = coupling[:, rows] + nt(side[...], near[rows, at["side_cols"]])
        y = (rhs[:, rows] - part) * inv[:, rows]
        x = y + (nn(one, third[:, rows]) + nn(two, both[:, rows]) + nn(mine_3[...], first[:, rows]))
        current[:, rows] = x
        x_out[:, rows] = x.astype(jnp.bfloat16)


def join_body(x, one, three, two, out):
    group = lax.axis_index("grp")
    for k, part in zip((0, 1, 3, 2), (x, one, three, two)):
        owner = group ^ k
        out[:, pl.ds(pl.multiple_of(owner * OWN, OWN), OWN)] = part[...]


def body(
    incident, self_term, near_field, history, ret_values, slot_row, slot_col, slot_delay, live_count
):
    count = lax.axis_size("patch")
    inv = self_term[None, :]
    chip = [(i, i ^ 1) for i in range(count)]
    links = [(i, i + 1) for i in range(1, count - 1, 2)]
    links = links + [(b, a) for a, b in links]
    beyond = [(i, i + 3) for i in range(1, count - 3, 2)]
    beyond = beyond + [(b, a) for a, b in beyond]
    product = 2 * OWN * OWN

    cross = lax.ppermute(history, "patch", links)
    side = lax.ppermute(history, "patch", chip)
    values = in_vmem(ret_values)
    codes = pltpu.SMEM((SLOTS + 2 * UNROLL,), jnp.int32)

    near, coupling, first, second, inner, inv, home_codes, far_codes = call(
        response_1_body,
        (pltpu.VMEM((OWN, EDGE + BLK), jnp.bfloat16), f32(WAVES, OWN), bf16(BLK, OWN), bf16(BLK, OWN),
         bf16(BLK, BLK), f32(1, OWN), codes, codes),
        [SMEM] + [HBM] * 6,
        (VMEM,) * 6 + (SMEM,) * 2,
        (live_count,) + tuple(in_hbm(x) for x in (slot_row, slot_col, slot_delay, inv, near_field, history)),
        product * 144,
        8 * 2**20,
        [
            pltpu.VMEM((OWN, BLK), jnp.bfloat16),
            pltpu.VMEM((WAVES, OWN), jnp.bfloat16),
            pltpu.SMEM((SLOTS,), jnp.int32),
            pltpu.SMEM((SLOTS,), jnp.int32),
            pltpu.SMEM((SLOTS,), jnp.int32),
            pltpu.SemaphoreType.DMA((6 + OWN // ROWS,)),
        ],
    )
    near = in_vmem(near)
    home_codes, far_codes = (pltpu.with_memory_space_constraint(x, pltpu.SMEM) for x in (home_codes, far_codes))
    both, inner, corners = call(
        response_2_body,
        (bf16(2 * BLK, OWN), bf16(2 * BLK, BLK), bf16(3 * BLK, BLK)),
        [VMEM] * 5,
        (VMEM,) * 3,
        (near, inv, first, second, lax.ppermute(inner, "patch", chip)),
        product * 16,
        2**20,
    )
    corners = lax.ppermute(corners, "patch", links)
    third = call(
        response_3_body,
        bf16(2 * BLK, OWN),
        [VMEM] * 4,
        VMEM,
        (near, inv, both, lax.ppermute(inner, "patch", chip)),
        product * 256,
        8 * 2**20,
    )
    acc = call(
        home_body,
        f32(RB, WAVES, BLK),
        [SMEM] + [VMEM] * 3,
        VMEM,
        (home_codes, values, in_vmem(history), in_vmem(side)),
        2 * 10**9,
        10 * 10**6,
    )
    rhs, x, inner = call(
        second_body,
        (f32(WAVES, OWN), bf16(WAVES, OWN), bf16(WAVES, BLK)),
        [SMEM] + [VMEM] * 8 + [HBM],
        (VMEM,) * 3,
        (far_codes, values, near, in_vmem(cross), in_vmem(side), acc, coupling, incident, inv, third),
        10**9,
        10**6,
        [pltpu.VMEM((RB, WAVES, BLK), jnp.float32)],
    )
    edge = lax.ppermute(inner, "patch", chip)
    coupling = call(own_body, f32(WAVES, OWN), [VMEM] * 2, VMEM, (x, near), product * 16, 8 * 2**20)
    y, far = call(
        side_body,
        (bf16(WAVES, OWN), bf16(WAVES, HALF)),
        [VMEM] * 6,
        (VMEM,) * 2,
        (near, edge, coupling, rhs, inv, x),
        product,
        2**19,
    )
    edge = lax.ppermute(y, "patch", chip)
    far = lax.ppermute(far, "patch", beyond)
    near_by = call(
        early_body,
        bf16(3 * WAVES, BLK),
        [VMEM] * 6,
        VMEM,
        (near, x, y, edge, rhs, inv),
        product,
        2**19,
    )
    near_by = lax.ppermute(near_by, "patch", links)
    y_3, inner = call(
        whole_body,
        (bf16(WAVES, OWN), bf16(WAVES, BLK)),
        [VMEM] * 5,
        (VMEM,) * 2,
        (near, y, edge, rhs, inv),
        product * 16,
        8 * 2**20,
    )
    edge = lax.ppermute(inner, "patch", chip)
    coupling = call(
        own_body, f32(WAVES, OWN), [VMEM] * 2, VMEM, (y_3, near), product * 16, 8 * 2**20
    )
    shared, mine_3 = call(
        edges_body,
        (bf16(2 * WAVES, BLK), bf16(WAVES, BLK)),
        [VMEM] * 6,
        (VMEM,) * 2,
        (near_by, far, corners, first, x, y),
        product // 100,
        2**17,
    )
    other = lax.ppermute(shared, "patch", chip)
    current, x = call(
        last_body,
        (f32(WAVES, OWN), bf16(WAVES, OWN)),
        [VMEM] * 11,
        (VMEM,) * 2,
        (near, edge, coupling, rhs, inv, shared, mine_3, other, first, both, third),
        product * 4,
        2**21,
    )
    turns = [
        lax.ppermute(x, "grp", [(i, i ^ k) for i in range(4)]) for k in (1, 3, 2)
    ]
    newest = call(
        join_body, bf16(WAVES, PATCH), [VMEM] * 4, VMEM, (x, *turns), 0, 2**20
    )
    return current, newest


def solution(mesh):
    placed = (
        P(None, ("patch", "grp")),
        P(("patch", "grp")),
        P(("patch", "grp"), None),
        P(None, None, "patch"),
        P(("patch", "grp"), None, None),
        P(("patch", "grp")),
        P(("patch", "grp")),
        P(("patch", "grp")),
        P(("patch", "grp")),
    )
    return jax.shard_map(
        body,
        mesh=mesh,
        in_specs=placed,
        out_specs=(P(None, ("patch", "grp")), P(None, "patch")),
        check_vma=False,
    )
```

```python
import jax
import jax.numpy as jnp
from jax import lax
from jax.experimental import pallas as pl
from jax.experimental.pallas import tpu as pltpu
from jax.sharding import PartitionSpec as P

BLK = 128
WAVES = 16
DELAYS = 8
SWEEPS = 4
RB = 16
SLOTS = 256
OWN = RB * BLK
EDGE = OWN + BLK
PATCH = 4 * OWN
COLS = PATCH // BLK
UNROLL = 32
DIRECT = 4
ROWS = 256
NT = (((1,), (1,)), ((), ()))

VMEM = pl.BlockSpec(memory_space=pltpu.VMEM)
HBM = pl.BlockSpec(memory_space=pl.ANY)
SMEM = pl.BlockSpec(memory_space=pltpu.SMEM)


def f32(*shape):
    return jax.ShapeDtypeStruct(shape, jnp.float32)


def bf16(*shape):
    return jax.ShapeDtypeStruct(shape, jnp.bfloat16)


def in_vmem(x):
    return pltpu.with_memory_space_constraint(x, pltpu.VMEM)


def in_hbm(x):
    return pltpu.with_memory_space_constraint(x, pltpu.HBM)


def call(body, out, ins, outs, args, flops, touched, scratch=()):
    return pl.pallas_call(
        body,
        out_shape=out,
        in_specs=ins,
        out_specs=outs,
        scratch_shapes=scratch,
        compiler_params=pltpu.CompilerParams(vmem_limit_bytes=16 * 2**20),
        cost_estimate=pl.CostEstimate(flops=flops, bytes_accessed=touched, transcendentals=0),
    )(*args)


def add_slots(count, codes, values, acc, block_of):
    def step(i, carry):
        found = []
        for j in range(0, UNROLL, 2):
            pair = []
            for k in (j, j + 1):
                at = i * UNROLL + k
                code = codes[at]
                block = block_of(code)
                block = jnp.where(at < count, block, jnp.zeros_like(block))
                pair.append((code, block))
            (code_a, a), (code_b, b) = pair
            zero = jnp.zeros_like(a)
            left = jnp.concatenate(
                [jnp.concatenate([a, zero], axis=1), jnp.concatenate([zero, b], axis=1)], axis=0
            )
            right = jnp.concatenate([values[code_a & 255], values[code_b & 255]], axis=1)
            both = lax.dot_general(left, right, NT, preferred_element_type=jnp.float32)
            found.append((code_a, both[:WAVES]))
            found.append((code_b, both[WAVES:]))
        for code, part in found:
            row = (code >> 8) & 15
            acc[row] = acc[row] + part
        return carry

    lax.fori_loop(0, (count + UNROLL - 1) // UNROLL, step, 0)


def own_coupling(x, near, out):
    for at in range(0, OWN, ROWS):
        rows = near[at : at + ROWS, BLK:EDGE]
        out[:, at : at + ROWS] = lax.dot_general(x, rows, NT, preferred_element_type=jnp.float32)


def edge_coupling(parity, cross, near_side, near):
    left = jnp.where(parity == 0, cross, near_side)
    right = jnp.where(parity == 0, near_side, cross)
    both = jnp.concatenate([left, right], axis=1)
    out = []
    for at in range(0, OWN, ROWS):
        rows = jnp.concatenate(
            [near[at : at + ROWS, :BLK], near[at : at + ROWS, EDGE:]], axis=1
        )
        out.append(lax.dot_general(both, rows, NT, preferred_element_type=jnp.float32))
    return out


def home_body(codes, values, own, side, after, acc):
    acc[...] = jnp.zeros_like(acc)

    def block_of(code):
        delay = (code >> 12) & 7
        at = pl.multiple_of(((code >> 15) & 63) * BLK, BLK)
        return jnp.where(
            ((code >> 21) & 1) == 1,
            side[delay, :, pl.ds(at, BLK)],
            own[delay, :, pl.ds(at, BLK)],
        )

    add_slots(codes[0], _Shifted(codes), values, acc, block_of)


def sort_slots(span, parity, limit, counts, slot_row, slot_col, slot_delay, home_codes, far_codes):
    home, far = counts
    for s in span:
        col = slot_col[s]
        third = jnp.where(col >= 2 * COLS, 2, jnp.where(col >= COLS, 1, 0))
        is_far = third == 2 * parity
        code = (
            s
            | (slot_row[s] << 8)
            | (slot_delay[s] << 12)
            | ((col - third * COLS) << 15)
            | (jnp.where(third == 1, 0, 1) << 21)
        )
        home_codes[1 + home] = code
        far_codes[1 + far] = code
        alive = jnp.where(s < limit, 1, 0)
        passed = jnp.where(is_far, alive, 0)
        home, far = home + alive - passed, far + passed
    return home, far


def close_lists(counts, home_codes, far_codes):
    home, far = counts
    home_codes[0] = home
    far_codes[0] = far

    def clear(k, carry):
        home_codes[1 + home + k] = 0
        far_codes[1 + far + k] = 0
        return carry

    lax.fori_loop(0, UNROLL, clear, 0)


class _Shifted:
    def __init__(self, ref):
        self.ref = ref

    def __getitem__(self, at):
        return self.ref[at + 1]


def core_parity():
    return lax.rem(lax.axis_index("patch"), 2)


def lanes(at):
    return pl.ds(pl.multiple_of(at, BLK), BLK)


def places():
    parity = core_parity()
    return {
        "cross_cols": lanes(parity * EDGE),
        "side_cols": lanes((1 - parity) * EDGE),
        "outer": lanes(parity * (OWN - BLK)),
        "inner": lanes((1 - parity) * (OWN - BLK)),
    }


def chunks():
    return [slice(at, at + ROWS) for at in range(0, OWN, ROWS)]


def spans():
    return [pl.ds(at, ROWS) for at in range(0, OWN, ROWS)]


def nt(a, b):
    return lax.dot_general(a, b, NT, preferred_element_type=jnp.float32)


def nn(a, b):
    return jnp.dot(a, b, preferred_element_type=jnp.float32)


def lists_body(
    live, row_hbm, col_hbm, delay_hbm, self_hbm, history, near_hbm,
    near, inv, newest, home_codes, far_codes, slot_row, slot_col, slot_delay, sems,
):
    start = pl.multiple_of(lax.axis_index("grp") * OWN, OWN)
    pairs = [
        (row_hbm, slot_row),
        (col_hbm, slot_col),
        (delay_hbm, slot_delay),
        (self_hbm, inv),
        (history.at[0, :, pl.ds(start, OWN)], newest),
    ] + [(near_hbm.at[rows], near.at[rows]) for rows in spans()]
    copies = [pltpu.make_async_copy(a, b, sems.at[i]) for i, (a, b) in enumerate(pairs)]
    for copy in copies:
        copy.start()
    for copy in copies[:5]:
        copy.wait()
    inv[...] = 1.0 / inv[...]
    parity, limit = core_parity(), live[0]

    def some(i, counts):
        return sort_slots(
            [i * 16 + k for k in range(16)], parity, limit, counts,
            slot_row, slot_col, slot_delay, home_codes, far_codes,
        )

    counts = lax.fori_loop(0, SLOTS // 16, some, (jnp.int32(0), jnp.int32(0)))
    close_lists(counts, home_codes, far_codes)
    for copy in copies[5:]:
        copy.wait()


def response_1_body(near, inv, newest, first, coupling, second, inner):
    at = places()
    eye = jnp.where(
        lax.broadcasted_iota(jnp.int32, (BLK, BLK), 0) == lax.broadcasted_iota(jnp.int32, (BLK, BLK), 1), 1.0, 0.0
    ).astype(jnp.bfloat16)
    for rows in chunks():
        first[:, rows] = (-nt(eye, near[rows, at["cross_cols"]]) * inv[:, rows]).astype(jnp.bfloat16)
    inner[...] = first[:, at["inner"]]
    both = jnp.concatenate([first[...], newest[...]], axis=0)
    for rows in chunks():
        made = nt(both, near[rows, BLK:EDGE])
        second[:, rows] = (-made[:BLK] * inv[:, rows]).astype(jnp.bfloat16)
        coupling[:, rows] = made[BLK:]


def response_2_body(near, inv, first, second, side, both, inner, corners):
    at = places()
    both[:BLK] = second[...]
    for rows in chunks():
        both[BLK:, rows] = (-nt(side[...], near[rows, at["side_cols"]]) * inv[:, rows]).astype(jnp.bfloat16)
    inner[...] = both[:, at["inner"]]
    corners[:BLK] = first[:, at["outer"]]
    corners[BLK:] = both[:, at["outer"]]


def response_3_body(near, inv, both, side, third):
    at = places()
    turned = jnp.concatenate([side[BLK:], side[:BLK]], axis=0)
    for rows in chunks():
        made = nt(both[...], near[rows, BLK:EDGE]) + nt(turned, near[rows, at["side_cols"]])
        third[:, rows] = (-made * inv[:, rows]).astype(jnp.bfloat16)


def parts_body(history, half, direct, sems):
    role = lax.rem(lax.axis_index("grp"), 2)
    copies = [
        pltpu.make_async_copy(history.at[pl.ds(DIRECT + 2 * role, 2)], half, sems.at[0]),
        pltpu.make_async_copy(history.at[pl.ds(0, DIRECT)], direct, sems.at[1]),
    ]
    for copy in copies:
        copy.start()
    for copy in copies:
        copy.wait()


def second_body(
    codes, values, near, cross, mine, other, side, acc, coupling, incident, inv, after,
    rhs, x_out, inner, total,
):
    parity, group = core_parity(), lax.axis_index("grp")
    role = lax.rem(group, 2)
    total[...] = acc[...]

    def block_of(code):
        delay = (code >> 12) & 7
        at = pl.multiple_of(((code >> 15) & 63) * BLK, BLK)
        low, half = delay & 1, (delay >> 1) & 1
        late = jnp.where(half == role, mine[low, :, pl.ds(at, BLK)], other[low, :, pl.ds(at, BLK)])
        return jnp.where(delay < DIRECT, cross[delay & (DIRECT - 1), :, pl.ds(at, BLK)], late)

    add_slots(codes[0], _Shifted(codes), values, total, block_of)
    for r in range(RB):
        at = slice(r * BLK, (r + 1) * BLK)
        rhs[:, at] = incident[:, at] - total[r]
    first = group * OWN
    last = group * OWN + OWN - BLK
    from_cross = cross[0, :, lanes(jnp.where(parity == 0, last, first))]
    from_side = side[0, :, lanes(jnp.where(parity == 0, first, last))]
    parts = edge_coupling(parity, from_cross, from_side, near)
    for rows, part in zip(chunks(), parts):
        x_out[:, rows] = ((rhs[:, rows] - (coupling[:, rows] + part)) * inv[:, rows]).astype(jnp.bfloat16)
    inner[...] = x_out[:, places()["inner"]]


def own_body(x, near, out):
    own_coupling(x[...], near, out)


def side_body(near, side, coupling, rhs, inv, x, y_out, far):
    at = places()
    for rows in chunks():
        part = coupling[:, rows] + nt(side[...], near[rows, at["side_cols"]])
        y_out[:, rows] = ((rhs[:, rows] - part) * inv[:, rows]).astype(jnp.bfloat16)
    far[:WAVES] = y_out[...]
    far[WAVES:] = x[...]


def early_body(near, x, y, side, rhs, inv, corners, near_by):
    at = places()
    rows = pl.ds(pl.multiple_of(core_parity() * (OWN - BLK), BLK), BLK)
    part = nt(y[...], near[rows, BLK:EDGE]) + nt(side[:WAVES, at["outer"]], near[rows, at["side_cols"]])
    third = (rhs[:, at["outer"]] - part) * inv[:, at["outer"]]
    near_by[:WAVES] = x[:, at["outer"]]
    near_by[WAVES : 2 * WAVES] = y[:, at["outer"]]
    near_by[2 * WAVES : 3 * WAVES] = third.astype(jnp.bfloat16)
    near_by[3 * WAVES :] = corners[...]


def whole_body(near, x, side, rhs, inv, y_out, inner):
    at = places()
    for rows in chunks():
        part = nt(x[...], near[rows, BLK:EDGE]) + nt(side[:WAVES, at["outer"]], near[rows, at["side_cols"]])
        y_out[:, rows] = ((rhs[:, rows] - part) * inv[:, rows]).astype(jnp.bfloat16)
    inner[...] = y_out[:, at["inner"]]


def edges_body(near_by, far, first, x, y, after, after_too, shared, third):
    at = places()
    one, mine = near_by[:WAVES], x[:, at["outer"]]
    mine_2 = y[:, at["outer"]].astype(jnp.float32) + nn(one, first[:, at["outer"]])
    corners = near_by[3 * WAVES :]
    two = near_by[WAVES : 2 * WAVES].astype(jnp.float32) + nn(mine, corners[:BLK])
    three = near_by[2 * WAVES : 3 * WAVES].astype(jnp.float32) + nn(mine, corners[BLK : 2 * BLK])
    three = three + nn(far[WAVES:, at["inner"]], corners[2 * BLK :]) + nn(mine_2.astype(jnp.bfloat16), corners[:BLK])
    shared[:WAVES] = one
    shared[WAVES:] = two.astype(jnp.bfloat16)
    third[...] = three.astype(jnp.bfloat16)


def own_part_body(near, side, coupling, rhs, inv, mine, mine_3, first, both, third, out):
    at = places()
    edges = jnp.concatenate([mine[:WAVES], mine[WAVES:]], axis=1)
    for rows in chunks():
        part = coupling[:, rows] + nt(side[...], near[rows, at["side_cols"]])
        response = jnp.concatenate([third[:BLK, rows], both[:BLK, rows]], axis=0)
        out[:, rows] = (rhs[:, rows] - part) * inv[:, rows] + (nn(edges, response) + nn(mine_3[...], first[:, rows]))


def last_body(partial, other, both, third, current, x_out):
    edges = jnp.concatenate([other[:WAVES], other[WAVES:]], axis=1)
    for rows in chunks():
        response = jnp.concatenate([third[BLK:, rows], both[BLK:, rows]], axis=0)
        x = partial[:, rows] + nn(edges, response)
        current[:, rows] = x
        x_out[:, rows] = x.astype(jnp.bfloat16)


def join_body(x, one, three, two, out):
    group = lax.axis_index("grp")
    for k, part in zip((0, 1, 3, 2), (x, one, three, two)):
        owner = group ^ k
        out[:, pl.ds(pl.multiple_of(owner * OWN, OWN), OWN)] = part[...]


def body(
    incident, self_term, near_field, history, ret_values, slot_row, slot_col, slot_delay, live_count
):
    count = lax.axis_size("patch")
    inv = self_term[None, :]
    chip = [(i, i ^ 1) for i in range(count)]
    links = [(i, i + 1) for i in range(1, count - 1, 2)]
    links = links + [(b, a) for a, b in links]
    beyond = [(i, i + 3) for i in range(1, count - 3, 2)]
    beyond = beyond + [(b, a) for a, b in beyond]
    product = 2 * OWN * OWN

    pairs = [
        (p * 4 + (g + p) % 4, p * 4 + ((g ^ 1) + p) % 4) for p in range(count) for g in range(4)
    ]
    half, direct = call(
        parts_body,
        (bf16(2, WAVES, PATCH), bf16(DIRECT, WAVES, PATCH)),
        [HBM],
        (HBM, HBM),
        (in_hbm(history),),
        1,
        3 * 2**20,
        [pltpu.SemaphoreType.DMA((2,))],
    )
    mine = lax.ppermute(half, "patch", links)
    cross = lax.ppermute(direct, "patch", links)
    side = lax.ppermute(history, "patch", chip)
    codes = pltpu.SMEM((SLOTS + 2 * UNROLL,), jnp.int32)

    near, inv, newest, home_codes, far_codes = call(
        lists_body,
        (pltpu.VMEM((OWN, EDGE + BLK), jnp.bfloat16), f32(1, OWN), bf16(WAVES, OWN), codes, codes),
        [SMEM] + [HBM] * 6,
        (VMEM,) * 3 + (SMEM,) * 2,
        (live_count,)
        + tuple(in_hbm(x) for x in (slot_row, slot_col, slot_delay, inv, history, near_field)),
        10**6,
        12 * 10**6,
        [
            pltpu.SMEM((SLOTS,), jnp.int32),
            pltpu.SMEM((SLOTS,), jnp.int32),
            pltpu.SMEM((SLOTS,), jnp.int32),
            pltpu.SemaphoreType.DMA((5 + OWN // ROWS,)),
        ],
    )
    near = in_vmem(near)
    mine, newest = lax.optimization_barrier((mine, newest))
    other = lax.ppermute(mine, ("patch", "grp"), pairs)
    home_codes, far_codes = (pltpu.with_memory_space_constraint(x, pltpu.SMEM) for x in (home_codes, far_codes))
    first, coupling, second, inner = call(
        response_1_body,
        (bf16(BLK, OWN), f32(WAVES, OWN), bf16(BLK, OWN), bf16(BLK, BLK)),
        [VMEM] * 3,
        (VMEM,) * 4,
        (near, inv, newest),
        product * 144,
        12 * 10**6,
    )
    values, own = in_vmem(ret_values), in_vmem(history)
    both, inner, corners = call(
        response_2_body,
        (bf16(2 * BLK, OWN), bf16(2 * BLK, BLK), bf16(3 * BLK, BLK)),
        [VMEM] * 5,
        (VMEM,) * 3,
        (near, inv, first, second, lax.ppermute(inner, "patch", chip)),
        product * 16,
        2**20,
    )
    third = call(
        response_3_body,
        bf16(2 * BLK, OWN),
        [VMEM] * 4,
        VMEM,
        (near, inv, both, lax.ppermute(inner, "patch", chip)),
        product * 256,
        8 * 2**20,
    )
    acc = call(
        home_body,
        f32(RB, WAVES, BLK),
        [SMEM] + [VMEM] * 3 + [HBM],
        VMEM,
        (home_codes, values, own, in_vmem(side), third),
        2 * 10**9,
        10 * 10**6,
    )
    rhs, x, inner = call(
        second_body,
        (f32(WAVES, OWN), bf16(WAVES, OWN), bf16(WAVES, BLK)),
        [SMEM] + [VMEM] * 10 + [HBM],
        (VMEM,) * 3,
        (far_codes, values, near, in_vmem(cross), in_vmem(mine), in_vmem(other), in_vmem(side), acc, coupling, incident, inv, third),
        10**9,
        10**6,
        [pltpu.VMEM((RB, WAVES, BLK), jnp.float32)],
    )
    edge = lax.ppermute(inner, "patch", chip)
    coupling = call(own_body, f32(WAVES, OWN), [VMEM] * 2, VMEM, (x, near), product * 16, 8 * 2**20)
    y, far = call(
        side_body,
        (bf16(WAVES, OWN), bf16(2 * WAVES, OWN)),
        [VMEM] * 6,
        (VMEM,) * 2,
        (near, edge, coupling, rhs, inv, x),
        product,
        2**19,
    )
    edge = lax.ppermute(far, "patch", chip)
    far = lax.ppermute(far, "patch", beyond)
    near_by = call(
        early_body,
        bf16(3 * WAVES + 3 * BLK, BLK),
        [VMEM] * 7,
        VMEM,
        (near, x, y, edge, rhs, inv, corners),
        product,
        2**19,
    )
    near_by = lax.ppermute(near_by, "patch", links)
    y_3, inner = call(
        whole_body,
        (bf16(WAVES, OWN), bf16(WAVES, BLK)),
        [VMEM] * 5,
        (VMEM,) * 2,
        (near, y, edge, rhs, inv),
        product * 16,
        8 * 2**20,
    )
    edge = lax.ppermute(inner, "patch", chip)
    coupling = call(
        own_body, f32(WAVES, OWN), [VMEM] * 2, VMEM, (y_3, near), product * 16, 8 * 2**20
    )
    shared, mine_3 = call(
        edges_body,
        (bf16(2 * WAVES, BLK), bf16(WAVES, BLK)),
        [VMEM] * 5 + [HBM] * 2,
        (VMEM,) * 2,
        (near_by, far, first, x, y, coupling, edge),
        product // 100,
        2**17,
    )
    other = lax.ppermute(shared, "patch", chip)
    partial = call(
        own_part_body,
        f32(WAVES, OWN),
        [VMEM] * 10,
        VMEM,
        (near, edge, coupling, rhs, inv, shared, mine_3, first, both, third),
        product * 3,
        2**21,
    )
    current, x = call(
        last_body,
        (f32(WAVES, OWN), bf16(WAVES, OWN)),
        [VMEM] * 4,
        (VMEM,) * 2,
        (partial, other, both, third),
        product * 2,
        2**20,
    )
    turns = [
        lax.ppermute(x, "grp", [(i, i ^ k) for i in range(4)]) for k in (1, 3, 2)
    ]
    newest = call(
        join_body, bf16(WAVES, PATCH), [VMEM] * 4, VMEM, (x, *turns), 0, 2**20
    )
    return current, newest


def solution(mesh):
    placed = (
        P(None, ("patch", "grp")),
        P(("patch", "grp")),
        P(("patch", "grp"), None),
        P(None, None, "patch"),
        P(("patch", "grp"), None, None),
        P(("patch", "grp")),
        P(("patch", "grp")),
        P(("patch", "grp")),
        P(("patch", "grp")),
    )
    return jax.shard_map(
        body,
        mesh=mesh,
        in_specs=placed,
        out_specs=(P(None, ("patch", "grp")), P(None, "patch")),
        check_vma=False,
    )
```

```python
import jax
import jax.numpy as jnp
from jax import lax
from jax.experimental import pallas as pl
from jax.experimental.pallas import tpu as pltpu
from jax.sharding import PartitionSpec as P

BLK = 128
WAVES = 16
DELAYS = 8
SWEEPS = 4
RB = 16
SLOTS = 256
OWN = RB * BLK
EDGE = OWN + BLK
PATCH = 4 * OWN
COLS = PATCH // BLK
UNROLL = 32
DIRECT = 4
ROWS = 256
NT = (((1,), (1,)), ((), ()))

VMEM = pl.BlockSpec(memory_space=pltpu.VMEM)
HBM = pl.BlockSpec(memory_space=pl.ANY)
SMEM = pl.BlockSpec(memory_space=pltpu.SMEM)


def f32(*shape):
    return jax.ShapeDtypeStruct(shape, jnp.float32)


def bf16(*shape):
    return jax.ShapeDtypeStruct(shape, jnp.bfloat16)


def in_vmem(x):
    return pltpu.with_memory_space_constraint(x, pltpu.VMEM)


def in_hbm(x):
    return pltpu.with_memory_space_constraint(x, pltpu.HBM)


def call(body, out, ins, outs, args, flops, touched, scratch=()):
    return pl.pallas_call(
        body,
        out_shape=out,
        in_specs=ins,
        out_specs=outs,
        scratch_shapes=scratch,
        compiler_params=pltpu.CompilerParams(vmem_limit_bytes=16 * 2**20),
        cost_estimate=pl.CostEstimate(flops=flops, bytes_accessed=touched, transcendentals=0),
    )(*args)


def add_slots(count, codes, values, acc, block_of):
    def step(i, carry):
        found = []
        for j in range(0, UNROLL, 2):
            pair = []
            for k in (j, j + 1):
                at = i * UNROLL + k
                code = codes[at]
                block = block_of(code)
                block = jnp.where(at < count, block, jnp.zeros_like(block))
                pair.append((code, block))
            (code_a, a), (code_b, b) = pair
            zero = jnp.zeros_like(a)
            left = jnp.concatenate(
                [jnp.concatenate([a, zero], axis=1), jnp.concatenate([zero, b], axis=1)], axis=0
            )
            right = jnp.concatenate([values[code_a & 255], values[code_b & 255]], axis=1)
            both = lax.dot_general(left, right, NT, preferred_element_type=jnp.float32)
            found.append((code_a, both[:WAVES]))
            found.append((code_b, both[WAVES:]))
        for code, part in found:
            row = (code >> 8) & 15
            acc[row] = acc[row] + part
        return carry

    lax.fori_loop(0, (count + UNROLL - 1) // UNROLL, step, 0)


def own_coupling(x, near, out):
    for at in range(0, OWN, ROWS):
        rows = near[at : at + ROWS, BLK:EDGE]
        out[:, at : at + ROWS] = lax.dot_general(x, rows, NT, preferred_element_type=jnp.float32)


def edge_coupling(parity, cross, near_side, near):
    left = jnp.where(parity == 0, cross, near_side)
    right = jnp.where(parity == 0, near_side, cross)
    both = jnp.concatenate([left, right], axis=1)
    out = []
    for at in range(0, OWN, ROWS):
        rows = jnp.concatenate(
            [near[at : at + ROWS, :BLK], near[at : at + ROWS, EDGE:]], axis=1
        )
        out.append(lax.dot_general(both, rows, NT, preferred_element_type=jnp.float32))
    return out


def home_body(codes, values, own, side, after, acc):
    acc[...] = jnp.zeros_like(acc)

    def block_of(code):
        delay = (code >> 12) & 7
        at = pl.multiple_of(((code >> 15) & 63) * BLK, BLK)
        return jnp.where(
            ((code >> 21) & 1) == 1,
            side[delay, :, pl.ds(at, BLK)],
            own[delay, :, pl.ds(at, BLK)],
        )

    add_slots(codes[0], _Shifted(codes), values, acc, block_of)


def sort_slots(span, parity, limit, counts, slot_row, slot_col, slot_delay, home_codes, far_codes):
    home, far = counts
    for s in span:
        col = slot_col[s]
        third = jnp.where(col >= 2 * COLS, 2, jnp.where(col >= COLS, 1, 0))
        is_far = third == 2 * parity
        code = (
            s
            | (slot_row[s] << 8)
            | (slot_delay[s] << 12)
            | ((col - third * COLS) << 15)
            | (jnp.where(third == 1, 0, 1) << 21)
        )
        home_codes[1 + home] = code
        far_codes[1 + far] = code
        alive = jnp.where(s < limit, 1, 0)
        passed = jnp.where(is_far, alive, 0)
        home, far = home + alive - passed, far + passed
    return home, far


def close_lists(counts, home_codes, far_codes):
    home, far = counts
    home_codes[0] = home
    far_codes[0] = far

    def clear(k, carry):
        home_codes[1 + home + k] = 0
        far_codes[1 + far + k] = 0
        return carry

    lax.fori_loop(0, UNROLL, clear, 0)


class _Shifted:
    def __init__(self, ref):
        self.ref = ref

    def __getitem__(self, at):
        return self.ref[at + 1]


def core_parity():
    return lax.rem(lax.axis_index("patch"), 2)


def lanes(at):
    return pl.ds(pl.multiple_of(at, BLK), BLK)


def places():
    parity = core_parity()
    return {
        "cross_cols": lanes(parity * EDGE),
        "side_cols": lanes((1 - parity) * EDGE),
        "outer": lanes(parity * (OWN - BLK)),
        "inner": lanes((1 - parity) * (OWN - BLK)),
    }


def chunks():
    return [slice(at, at + ROWS) for at in range(0, OWN, ROWS)]


def spans():
    return [pl.ds(at, ROWS) for at in range(0, OWN, ROWS)]


def nt(a, b):
    return lax.dot_general(a, b, NT, preferred_element_type=jnp.float32)


def nn(a, b):
    return jnp.dot(a, b, preferred_element_type=jnp.float32)


def lists_body(
    live, row_hbm, col_hbm, delay_hbm, self_hbm, history, near_hbm,
    near, inv, newest, home_codes, far_codes, slot_row, slot_col, slot_delay, sems,
):
    start = pl.multiple_of(lax.axis_index("grp") * OWN, OWN)
    pairs = [
        (row_hbm, slot_row),
        (col_hbm, slot_col),
        (delay_hbm, slot_delay),
        (self_hbm, inv),
        (history.at[0, :, pl.ds(start, OWN)], newest),
    ] + [(near_hbm.at[rows], near.at[rows]) for rows in spans()]
    copies = [pltpu.make_async_copy(a, b, sems.at[i]) for i, (a, b) in enumerate(pairs)]
    for copy in copies:
        copy.start()
    for copy in copies[:5]:
        copy.wait()
    inv[...] = 1.0 / inv[...]
    parity, limit = core_parity(), live[0]

    def some(i, counts):
        return sort_slots(
            [i * 16 + k for k in range(16)], parity, limit, counts,
            slot_row, slot_col, slot_delay, home_codes, far_codes,
        )

    counts = lax.fori_loop(0, SLOTS // 16, some, (jnp.int32(0), jnp.int32(0)))
    close_lists(counts, home_codes, far_codes)
    for copy in copies[5:]:
        copy.wait()


def response_1_body(near, inv, newest, first, coupling, second, inner):
    at = places()
    eye = jnp.where(
        lax.broadcasted_iota(jnp.int32, (BLK, BLK), 0) == lax.broadcasted_iota(jnp.int32, (BLK, BLK), 1), 1.0, 0.0
    ).astype(jnp.bfloat16)
    for rows in chunks():
        first[:, rows] = (-nt(eye, near[rows, at["cross_cols"]]) * inv[:, rows]).astype(jnp.bfloat16)
    both = jnp.concatenate([first[...], newest[...]], axis=0)
    for rows in chunks():
        made = nt(both, near[rows, BLK:EDGE])
        second[:, rows] = (-made[:BLK] * inv[:, rows]).astype(jnp.bfloat16)
        coupling[:, rows] = made[BLK:]
    rows = pl.ds(pl.multiple_of((1 - core_parity()) * (OWN - BLK), BLK), BLK)
    step = -nt(eye, near[rows, at["side_cols"]]) * inv[:, at["inner"]]
    inner[:BLK] = first[:, at["inner"]]
    inner[BLK : 2 * BLK] = second[:, at["inner"]]
    inner[2 * BLK :] = step.astype(jnp.bfloat16)


def response_23_body(near, inv, first, second, side, both, third, corners):
    at = places()
    both[:BLK] = second[...]
    for rows in chunks():
        made = nt(side[:BLK], near[rows, at["side_cols"]])
        both[BLK:, rows] = (-made * inv[:, rows]).astype(jnp.bfloat16)
    crossed = nn(first[:, at["inner"]], side[2 * BLK :]).astype(jnp.bfloat16)
    turned = jnp.concatenate([crossed, side[BLK : 2 * BLK]], axis=0)
    for rows in chunks():
        made = nt(both[...], near[rows, BLK:EDGE]) + nt(turned, near[rows, at["side_cols"]])
        third[:, rows] = (-made * inv[:, rows]).astype(jnp.bfloat16)
    corners[:BLK] = first[:, at["outer"]]
    corners[BLK:] = both[:, at["outer"]]


def parts_body(history, half, direct, sems):
    role = lax.rem(lax.axis_index("grp"), 2)
    copies = [
        pltpu.make_async_copy(history.at[pl.ds(DIRECT + 2 * role, 2)], half, sems.at[0]),
        pltpu.make_async_copy(history.at[pl.ds(0, DIRECT)], direct, sems.at[1]),
    ]
    for copy in copies:
        copy.start()
    for copy in copies:
        copy.wait()


def second_body(
    codes, values, near, cross, mine, other, side, acc, coupling, incident, inv, after,
    rhs, x_out, inner, total,
):
    parity, group = core_parity(), lax.axis_index("grp")
    role = lax.rem(group, 2)
    total[...] = acc[...]

    def block_of(code):
        delay = (code >> 12) & 7
        at = pl.multiple_of(((code >> 15) & 63) * BLK, BLK)
        low, half = delay & 1, (delay >> 1) & 1
        late = jnp.where(half == role, mine[low, :, pl.ds(at, BLK)], other[low, :, pl.ds(at, BLK)])
        return jnp.where(delay < DIRECT, cross[delay & (DIRECT - 1), :, pl.ds(at, BLK)], late)

    add_slots(codes[0], _Shifted(codes), values, total, block_of)
    for r in range(RB):
        at = slice(r * BLK, (r + 1) * BLK)
        rhs[:, at] = incident[:, at] - total[r]
    first = group * OWN
    last = group * OWN + OWN - BLK
    from_cross = cross[0, :, lanes(jnp.where(parity == 0, last, first))]
    from_side = side[0, :, lanes(jnp.where(parity == 0, first, last))]
    parts = edge_coupling(parity, from_cross, from_side, near)
    for rows, part in zip(chunks(), parts):
        x_out[:, rows] = ((rhs[:, rows] - (coupling[:, rows] + part)) * inv[:, rows]).astype(jnp.bfloat16)
    inner[...] = x_out[:, places()["inner"]]


def own_body(x, near, out):
    own_coupling(x[...], near, out)


def side_body(near, side, coupling, rhs, inv, x, y_out, far):
    at = places()
    for rows in chunks():
        part = coupling[:, rows] + nt(side[...], near[rows, at["side_cols"]])
        y_out[:, rows] = ((rhs[:, rows] - part) * inv[:, rows]).astype(jnp.bfloat16)
    far[:WAVES] = y_out[...]
    far[WAVES:] = x[...]


def early_body(near, x, y, side, rhs, inv, corners, near_by):
    at = places()
    rows = pl.ds(pl.multiple_of(core_parity() * (OWN - BLK), BLK), BLK)
    part = nt(y[...], near[rows, BLK:EDGE]) + nt(side[:WAVES, at["outer"]], near[rows, at["side_cols"]])
    third = (rhs[:, at["outer"]] - part) * inv[:, at["outer"]]
    near_by[:WAVES] = x[:, at["outer"]]
    near_by[WAVES : 2 * WAVES] = y[:, at["outer"]]
    near_by[2 * WAVES : 3 * WAVES] = third.astype(jnp.bfloat16)
    near_by[3 * WAVES :] = corners[...]


def whole_body(near, x, side, rhs, inv, y_out, inner):
    at = places()
    for rows in chunks():
        part = nt(x[...], near[rows, BLK:EDGE]) + nt(side[:WAVES, at["outer"]], near[rows, at["side_cols"]])
        y_out[:, rows] = ((rhs[:, rows] - part) * inv[:, rows]).astype(jnp.bfloat16)
    inner[...] = y_out[:, at["inner"]]


def edges_body(near_by, far, first, x, y, after, after_too, shared, third):
    at = places()
    one, mine = near_by[:WAVES], x[:, at["outer"]]
    mine_2 = y[:, at["outer"]].astype(jnp.float32) + nn(one, first[:, at["outer"]])
    corners = near_by[3 * WAVES :]
    two = near_by[WAVES : 2 * WAVES].astype(jnp.float32) + nn(mine, corners[:BLK])
    three = near_by[2 * WAVES : 3 * WAVES].astype(jnp.float32) + nn(mine, corners[BLK : 2 * BLK])
    three = three + nn(far[WAVES:, at["inner"]], corners[2 * BLK :]) + nn(mine_2.astype(jnp.bfloat16), corners[:BLK])
    shared[:WAVES] = one
    shared[WAVES:] = two.astype(jnp.bfloat16)
    third[...] = three.astype(jnp.bfloat16)


def own_part_body(near, side, coupling, rhs, inv, mine, mine_3, first, both, third, out):
    at = places()
    edges = jnp.concatenate([mine[:WAVES], mine[WAVES:]], axis=1)
    for rows in chunks():
        part = coupling[:, rows] + nt(side[...], near[rows, at["side_cols"]])
        response = jnp.concatenate([third[:BLK, rows], both[:BLK, rows]], axis=0)
        out[:, rows] = (rhs[:, rows] - part) * inv[:, rows] + (nn(edges, response) + nn(mine_3[...], first[:, rows]))


def last_body(partial, other, both, third, current, x_out):
    edges = jnp.concatenate([other[:WAVES], other[WAVES:]], axis=1)
    for rows in chunks():
        response = jnp.concatenate([third[BLK:, rows], both[BLK:, rows]], axis=0)
        x = partial[:, rows] + nn(edges, response)
        current[:, rows] = x
        x_out[:, rows] = x.astype(jnp.bfloat16)


def join_body(x, one, three, two, out, sems):
    group = lax.axis_index("grp")
    copies = [
        pltpu.make_async_copy(
            part, out.at[:, pl.ds(pl.multiple_of((group ^ k) * OWN, OWN), OWN)], sems.at[k]
        )
        for k, part in zip((0, 1, 3, 2), (x, one, three, two))
    ]
    for copy in copies:
        copy.start()
    for copy in copies:
        copy.wait()


def body(
    incident, self_term, near_field, history, ret_values, slot_row, slot_col, slot_delay, live_count
):
    count = lax.axis_size("patch")
    inv = self_term[None, :]
    chip = [(i, i ^ 1) for i in range(count)]
    links = [(i, i + 1) for i in range(1, count - 1, 2)]
    links = links + [(b, a) for a, b in links]
    beyond = [(i, i + 3) for i in range(1, count - 3, 2)]
    beyond = beyond + [(b, a) for a, b in beyond]
    product = 2 * OWN * OWN

    pairs = [
        (p * 4 + (g + p) % 4, p * 4 + ((g ^ 1) + p) % 4) for p in range(count) for g in range(4)
    ]
    half, direct = call(
        parts_body,
        (bf16(2, WAVES, PATCH), bf16(DIRECT, WAVES, PATCH)),
        [HBM],
        (HBM, HBM),
        (in_hbm(history),),
        1,
        3 * 2**20,
        [pltpu.SemaphoreType.DMA((2,))],
    )
    mine = lax.ppermute(half, "patch", links)
    cross = lax.ppermute(direct, "patch", links)
    side = lax.ppermute(history, "patch", chip)
    codes = pltpu.SMEM((SLOTS + 2 * UNROLL,), jnp.int32)

    near, inv, newest, home_codes, far_codes = call(
        lists_body,
        (pltpu.VMEM((OWN, EDGE + BLK), jnp.bfloat16), f32(1, OWN), bf16(WAVES, OWN), codes, codes),
        [SMEM] + [HBM] * 6,
        (VMEM,) * 3 + (SMEM,) * 2,
        (live_count,)
        + tuple(in_hbm(x) for x in (slot_row, slot_col, slot_delay, inv, history, near_field)),
        10**6,
        12 * 10**6,
        [
            pltpu.SMEM((SLOTS,), jnp.int32),
            pltpu.SMEM((SLOTS,), jnp.int32),
            pltpu.SMEM((SLOTS,), jnp.int32),
            pltpu.SemaphoreType.DMA((5 + OWN // ROWS,)),
        ],
    )
    near = in_vmem(near)
    mine, newest = lax.optimization_barrier((mine, newest))
    other = lax.ppermute(mine, ("patch", "grp"), pairs)
    home_codes, far_codes = (pltpu.with_memory_space_constraint(x, pltpu.SMEM) for x in (home_codes, far_codes))
    first, coupling, second, inner = call(
        response_1_body,
        (bf16(BLK, OWN), f32(WAVES, OWN), bf16(BLK, OWN), bf16(3 * BLK, BLK)),
        [VMEM] * 3,
        (VMEM,) * 4,
        (near, inv, newest),
        product * 144,
        12 * 10**6,
    )
    values, own = in_vmem(ret_values), in_vmem(history)
    both, third, corners = call(
        response_23_body,
        (bf16(2 * BLK, OWN), bf16(2 * BLK, OWN), bf16(3 * BLK, BLK)),
        [VMEM] * 5,
        (VMEM,) * 3,
        (near, inv, first, second, lax.ppermute(inner, "patch", chip)),
        product * 256,
        8 * 2**20,
    )
    acc = call(
        home_body,
        f32(RB, WAVES, BLK),
        [SMEM] + [VMEM] * 3 + [HBM],
        VMEM,
        (home_codes, values, own, in_vmem(side), third),
        2 * 10**9,
        10 * 10**6,
    )
    rhs, x, inner = call(
        second_body,
        (f32(WAVES, OWN), bf16(WAVES, OWN), bf16(WAVES, BLK)),
        [SMEM] + [VMEM] * 10 + [HBM],
        (VMEM,) * 3,
        (far_codes, values, near, in_vmem(cross), in_vmem(mine), in_vmem(other), in_vmem(side), acc, coupling, incident, inv, third),
        10**9,
        10**6,
        [pltpu.VMEM((RB, WAVES, BLK), jnp.float32)],
    )
    edge = lax.ppermute(inner, "patch", chip)
    coupling = call(own_body, f32(WAVES, OWN), [VMEM] * 2, VMEM, (x, near), product * 16, 8 * 2**20)
    y, far = call(
        side_body,
        (bf16(WAVES, OWN), bf16(2 * WAVES, OWN)),
        [VMEM] * 6,
        (VMEM,) * 2,
        (near, edge, coupling, rhs, inv, x),
        product,
        2**19,
    )
    edge = lax.ppermute(far, "patch", chip)
    far = lax.ppermute(far, "patch", beyond)
    near_by = call(
        early_body,
        bf16(3 * WAVES + 3 * BLK, BLK),
        [VMEM] * 7,
        VMEM,
        (near, x, y, edge, rhs, inv, corners),
        product,
        2**19,
    )
    near_by = lax.ppermute(near_by, "patch", links)
    y_3, inner = call(
        whole_body,
        (bf16(WAVES, OWN), bf16(WAVES, BLK)),
        [VMEM] * 5,
        (VMEM,) * 2,
        (near, y, edge, rhs, inv),
        product * 16,
        8 * 2**20,
    )
    edge = lax.ppermute(inner, "patch", chip)
    coupling = call(
        own_body, f32(WAVES, OWN), [VMEM] * 2, VMEM, (y_3, near), product * 16, 8 * 2**20
    )
    shared, mine_3 = call(
        edges_body,
        (bf16(2 * WAVES, BLK), bf16(WAVES, BLK)),
        [VMEM] * 5 + [HBM] * 2,
        (VMEM,) * 2,
        (near_by, far, first, x, y, coupling, edge),
        product // 100,
        2**17,
    )
    other = lax.ppermute(shared, "patch", chip)
    partial = call(
        own_part_body,
        f32(WAVES, OWN),
        [VMEM] * 10,
        VMEM,
        (near, edge, coupling, rhs, inv, shared, mine_3, first, both, third),
        product * 3,
        2**21,
    )
    current, x = call(
        last_body,
        (pltpu.VMEM((WAVES, OWN), jnp.float32), bf16(WAVES, OWN)),
        [VMEM] * 4,
        (VMEM,) * 2,
        (partial, other, both, third),
        product * 2,
        2**20,
    )
    turns = [
        lax.ppermute(x, "grp", [(i, i ^ k) for i in range(4)]) for k in (1, 3, 2)
    ]
    newest = call(
        join_body,
        bf16(WAVES, PATCH),
        [VMEM] * 4,
        HBM,
        (x, *turns),
        0,
        2**20,
        [pltpu.SemaphoreType.DMA((4,))],
    )
    return current, newest


def solution(mesh):
    placed = (
        P(None, ("patch", "grp")),
        P(("patch", "grp")),
        P(("patch", "grp"), None),
        P(None, None, "patch"),
        P(("patch", "grp"), None, None),
        P(("patch", "grp")),
        P(("patch", "grp")),
        P(("patch", "grp")),
        P(("patch", "grp")),
    )
    return jax.shard_map(
        body,
        mesh=mesh,
        in_specs=placed,
        out_specs=(P(None, ("patch", "grp")), P(None, "patch")),
        check_vma=False,
    )
```

```python
import jax
import jax.numpy as jnp
from jax import lax
from jax.experimental import pallas as pl
from jax.experimental.pallas import tpu as pltpu
from jax.sharding import PartitionSpec as P

BLK = 128
WAVES = 16
DELAYS = 8
SWEEPS = 4
RB = 16
SLOTS = 256
OWN = RB * BLK
EDGE = OWN + BLK
PATCH = 4 * OWN
COLS = PATCH // BLK
UNROLL = 48
DIRECT = 4
ROWS = 256
NT = (((1,), (1,)), ((), ()))

VMEM = pl.BlockSpec(memory_space=pltpu.VMEM)
HBM = pl.BlockSpec(memory_space=pl.ANY)
SMEM = pl.BlockSpec(memory_space=pltpu.SMEM)


def f32(*shape):
    return jax.ShapeDtypeStruct(shape, jnp.float32)


def bf16(*shape):
    return jax.ShapeDtypeStruct(shape, jnp.bfloat16)


def in_vmem(x):
    return pltpu.with_memory_space_constraint(x, pltpu.VMEM)


def in_hbm(x):
    return pltpu.with_memory_space_constraint(x, pltpu.HBM)


def call(body, out, ins, outs, args, flops, touched, scratch=()):
    return pl.pallas_call(
        body,
        out_shape=out,
        in_specs=ins,
        out_specs=outs,
        scratch_shapes=scratch,
        compiler_params=pltpu.CompilerParams(vmem_limit_bytes=16 * 2**20),
        cost_estimate=pl.CostEstimate(flops=flops, bytes_accessed=touched, transcendentals=0),
    )(*args)


def add_slots(count, codes, values, acc, block_of):
    def step(i, carry):
        found = []
        for j in range(0, UNROLL, 2):
            pair = []
            for k in (j, j + 1):
                at = i * UNROLL + k
                code = codes[at]
                block = block_of(code)
                block = jnp.where(at < count, block, jnp.zeros_like(block))
                pair.append((code, block))
            (code_a, a), (code_b, b) = pair
            zero = jnp.zeros_like(a)
            left = jnp.concatenate(
                [jnp.concatenate([a, zero], axis=1), jnp.concatenate([zero, b], axis=1)], axis=0
            )
            right = jnp.concatenate([values[code_a & 255], values[code_b & 255]], axis=1)
            both = lax.dot_general(left, right, NT, preferred_element_type=jnp.float32)
            found.append((code_a, both[:WAVES]))
            found.append((code_b, both[WAVES:]))
        for code, part in found:
            row = (code >> 8) & 15
            acc[row] = acc[row] + part
        return carry

    lax.fori_loop(0, (count + UNROLL - 1) // UNROLL, step, 0)


def own_coupling(x, near, out):
    for at in range(0, OWN, ROWS):
        rows = near[at : at + ROWS, BLK:EDGE]
        out[:, at : at + ROWS] = lax.dot_general(x, rows, NT, preferred_element_type=jnp.float32)


def edge_coupling(parity, cross, near_side, near):
    left = jnp.where(parity == 0, cross, near_side)
    right = jnp.where(parity == 0, near_side, cross)
    both = jnp.concatenate([left, right], axis=1)
    out = []
    for at in range(0, OWN, ROWS):
        rows = jnp.concatenate(
            [near[at : at + ROWS, :BLK], near[at : at + ROWS, EDGE:]], axis=1
        )
        out.append(lax.dot_general(both, rows, NT, preferred_element_type=jnp.float32))
    return out


def home_body(codes, values, own, side, after, acc):
    acc[...] = jnp.zeros_like(acc)

    def block_of(code):
        delay = (code >> 12) & 7
        at = pl.multiple_of(((code >> 15) & 63) * BLK, BLK)
        return jnp.where(
            ((code >> 21) & 1) == 1,
            side[delay, :, pl.ds(at, BLK)],
            own[delay, :, pl.ds(at, BLK)],
        )

    add_slots(codes[0], _Shifted(codes), values, acc, block_of)


def sort_slots(span, parity, limit, counts, slot_row, slot_col, slot_delay, home_codes, far_codes):
    home, far = counts
    for s in span:
        col = slot_col[s]
        third = jnp.where(col >= 2 * COLS, 2, jnp.where(col >= COLS, 1, 0))
        is_far = third == 2 * parity
        code = (
            s
            | (slot_row[s] << 8)
            | (slot_delay[s] << 12)
            | ((col - third * COLS) << 15)
            | (jnp.where(third == 1, 0, 1) << 21)
        )
        home_codes[1 + home] = code
        far_codes[1 + far] = code
        alive = jnp.where(s < limit, 1, 0)
        passed = jnp.where(is_far, alive, 0)
        home, far = home + alive - passed, far + passed
    return home, far


def close_lists(counts, home_codes, far_codes):
    home, far = counts
    home_codes[0] = home
    far_codes[0] = far

    def clear(k, carry):
        home_codes[1 + home + k] = 0
        far_codes[1 + far + k] = 0
        return carry

    lax.fori_loop(0, UNROLL, clear, 0)


class _Shifted:
    def __init__(self, ref):
        self.ref = ref

    def __getitem__(self, at):
        return self.ref[at + 1]


def core_parity():
    return lax.rem(lax.axis_index("patch"), 2)


def lanes(at):
    return pl.ds(pl.multiple_of(at, BLK), BLK)


def places():
    parity = core_parity()
    return {
        "cross_cols": lanes(parity * EDGE),
        "side_cols": lanes((1 - parity) * EDGE),
        "outer": lanes(parity * (OWN - BLK)),
        "inner": lanes((1 - parity) * (OWN - BLK)),
    }


def chunks():
    return [slice(at, at + ROWS) for at in range(0, OWN, ROWS)]


def spans():
    return [pl.ds(at, ROWS) for at in range(0, OWN, ROWS)]


def nt(a, b):
    return lax.dot_general(a, b, NT, preferred_element_type=jnp.float32)


def nn(a, b):
    return jnp.dot(a, b, preferred_element_type=jnp.float32)


def lists_body(
    live, row_hbm, col_hbm, delay_hbm, self_hbm, history, near_hbm,
    near, inv, newest, home_codes, far_codes, slot_row, slot_col, slot_delay, sems,
):
    start = pl.multiple_of(lax.axis_index("grp") * OWN, OWN)
    pairs = [
        (row_hbm, slot_row),
        (col_hbm, slot_col),
        (delay_hbm, slot_delay),
        (self_hbm, inv),
        (history.at[0, :, pl.ds(start, OWN)], newest),
    ] + [(near_hbm.at[rows], near.at[rows]) for rows in spans()]
    copies = [pltpu.make_async_copy(a, b, sems.at[i]) for i, (a, b) in enumerate(pairs)]
    for copy in copies:
        copy.start()
    for copy in copies[:5]:
        copy.wait()
    inv[...] = 1.0 / inv[...]
    parity, limit = core_parity(), live[0]

    def some(i, counts):
        return sort_slots(
            [i * 16 + k for k in range(16)], parity, limit, counts,
            slot_row, slot_col, slot_delay, home_codes, far_codes,
        )

    counts = lax.fori_loop(0, SLOTS // 16, some, (jnp.int32(0), jnp.int32(0)))
    close_lists(counts, home_codes, far_codes)
    for copy in copies[5:]:
        copy.wait()


def response_1_body(near, inv, newest, first, coupling, second, inner):
    at = places()
    eye = jnp.where(
        lax.broadcasted_iota(jnp.int32, (BLK, BLK), 0) == lax.broadcasted_iota(jnp.int32, (BLK, BLK), 1), 1.0, 0.0
    ).astype(jnp.bfloat16)
    for rows in chunks():
        first[:, rows] = (-nt(eye, near[rows, at["cross_cols"]]) * inv[:, rows]).astype(jnp.bfloat16)
    both = jnp.concatenate([first[...], newest[...]], axis=0)
    for rows in chunks():
        made = nt(both, near[rows, BLK:EDGE])
        second[:, rows] = (-made[:BLK] * inv[:, rows]).astype(jnp.bfloat16)
        coupling[:, rows] = made[BLK:]
    rows = pl.ds(pl.multiple_of((1 - core_parity()) * (OWN - BLK), BLK), BLK)
    step = -nt(eye, near[rows, at["side_cols"]]) * inv[:, at["inner"]]
    inner[:BLK] = first[:, at["inner"]]
    inner[BLK : 2 * BLK] = second[:, at["inner"]]
    inner[2 * BLK :] = step.astype(jnp.bfloat16)


def response_23_body(near, inv, first, second, side, both, third, corners):
    at = places()
    both[:BLK] = second[...]
    for rows in chunks():
        made = nt(side[:BLK], near[rows, at["side_cols"]])
        both[BLK:, rows] = (-made * inv[:, rows]).astype(jnp.bfloat16)
    crossed = nn(first[:, at["inner"]], side[2 * BLK :]).astype(jnp.bfloat16)
    turned = jnp.concatenate([crossed, side[BLK : 2 * BLK]], axis=0)
    for rows in chunks():
        made = nt(both[...], near[rows, BLK:EDGE]) + nt(turned, near[rows, at["side_cols"]])
        third[:, rows] = (-made * inv[:, rows]).astype(jnp.bfloat16)
    corners[:BLK] = first[:, at["outer"]]
    corners[BLK:] = both[:, at["outer"]]


def parts_body(history, half, direct, sems):
    role = lax.rem(lax.axis_index("grp"), 2)
    copies = [
        pltpu.make_async_copy(history.at[pl.ds(DIRECT + 2 * role, 2)], half, sems.at[0]),
        pltpu.make_async_copy(history.at[pl.ds(0, DIRECT)], direct, sems.at[1]),
    ]
    for copy in copies:
        copy.start()
    for copy in copies:
        copy.wait()


def second_body(
    codes, values, near, cross, mine, other, side, acc, coupling, incident, inv, after,
    rhs, x_out, inner, total,
):
    parity, group = core_parity(), lax.axis_index("grp")
    role = lax.rem(group, 2)
    total[...] = acc[...]

    def block_of(code):
        delay = (code >> 12) & 7
        at = pl.multiple_of(((code >> 15) & 63) * BLK, BLK)
        low, half = delay & 1, (delay >> 1) & 1
        late = jnp.where(half == role, mine[low, :, pl.ds(at, BLK)], other[low, :, pl.ds(at, BLK)])
        return jnp.where(delay < DIRECT, cross[delay & (DIRECT - 1), :, pl.ds(at, BLK)], late)

    add_slots(codes[0], _Shifted(codes), values, total, block_of)
    for r in range(RB):
        at = slice(r * BLK, (r + 1) * BLK)
        rhs[:, at] = incident[:, at] - total[r]
    first = group * OWN
    last = group * OWN + OWN - BLK
    from_cross = cross[0, :, lanes(jnp.where(parity == 0, last, first))]
    from_side = side[0, :, lanes(jnp.where(parity == 0, first, last))]
    parts = edge_coupling(parity, from_cross, from_side, near)
    for rows, part in zip(chunks(), parts):
        x_out[:, rows] = ((rhs[:, rows] - (coupling[:, rows] + part)) * inv[:, rows]).astype(jnp.bfloat16)
    inner[...] = x_out[:, places()["inner"]]


def own_body(x, near, out):
    own_coupling(x[...], near, out)


def side_body(near, side, coupling, rhs, inv, x, y_out, far):
    at = places()
    for rows in chunks():
        part = coupling[:, rows] + nt(side[...], near[rows, at["side_cols"]])
        y_out[:, rows] = ((rhs[:, rows] - part) * inv[:, rows]).astype(jnp.bfloat16)
    far[:WAVES] = y_out[...]
    far[WAVES:] = x[...]


def early_body(near, x, y, side, rhs, inv, corners, near_by):
    at = places()
    rows = pl.ds(pl.multiple_of(core_parity() * (OWN - BLK), BLK), BLK)
    part = nt(y[...], near[rows, BLK:EDGE]) + nt(side[:WAVES, at["outer"]], near[rows, at["side_cols"]])
    third = (rhs[:, at["outer"]] - part) * inv[:, at["outer"]]
    near_by[:WAVES] = x[:, at["outer"]]
    near_by[WAVES : 2 * WAVES] = y[:, at["outer"]]
    near_by[2 * WAVES : 3 * WAVES] = third.astype(jnp.bfloat16)
    near_by[3 * WAVES :] = corners[...]


def whole_body(near, x, side, rhs, inv, y_out, inner):
    at = places()
    for rows in chunks():
        part = nt(x[...], near[rows, BLK:EDGE]) + nt(side[:WAVES, at["outer"]], near[rows, at["side_cols"]])
        y_out[:, rows] = ((rhs[:, rows] - part) * inv[:, rows]).astype(jnp.bfloat16)
    inner[...] = y_out[:, at["inner"]]


def edges_body(near_by, far, first, x, y, after, after_too, shared, third):
    at = places()
    one, mine = near_by[:WAVES], x[:, at["outer"]]
    mine_2 = y[:, at["outer"]].astype(jnp.float32) + nn(one, first[:, at["outer"]])
    corners = near_by[3 * WAVES :]
    two = near_by[WAVES : 2 * WAVES].astype(jnp.float32) + nn(mine, corners[:BLK])
    three = near_by[2 * WAVES : 3 * WAVES].astype(jnp.float32) + nn(mine, corners[BLK : 2 * BLK])
    three = three + nn(far[WAVES:, at["inner"]], corners[2 * BLK :]) + nn(mine_2.astype(jnp.bfloat16), corners[:BLK])
    shared[:WAVES] = one
    shared[WAVES:] = two.astype(jnp.bfloat16)
    third[...] = three.astype(jnp.bfloat16)


def own_part_body(near, side, coupling, rhs, inv, mine, mine_3, first, both, third, out):
    at = places()
    edges = jnp.concatenate([mine[:WAVES], mine[WAVES:]], axis=1)
    for rows in chunks():
        part = coupling[:, rows] + nt(side[...], near[rows, at["side_cols"]])
        response = jnp.concatenate([third[:BLK, rows], both[:BLK, rows]], axis=0)
        out[:, rows] = (rhs[:, rows] - part) * inv[:, rows] + (nn(edges, response) + nn(mine_3[...], first[:, rows]))


def last_body(partial, other, both, third, current, x_out):
    edges = jnp.concatenate([other[:WAVES], other[WAVES:]], axis=1)
    for rows in chunks():
        response = jnp.concatenate([third[BLK:, rows], both[BLK:, rows]], axis=0)
        x = partial[:, rows] + nn(edges, response)
        current[:, rows] = x
        x_out[:, rows] = x.astype(jnp.bfloat16)


def join_body(x, one, three, two, out, sems):
    group = lax.axis_index("grp")
    copies = [
        pltpu.make_async_copy(
            part, out.at[:, pl.ds(pl.multiple_of((group ^ k) * OWN, OWN), OWN)], sems.at[k]
        )
        for k, part in zip((0, 1, 3, 2), (x, one, three, two))
    ]
    for copy in copies:
        copy.start()
    for copy in copies:
        copy.wait()


def body(
    incident, self_term, near_field, history, ret_values, slot_row, slot_col, slot_delay, live_count
):
    count = lax.axis_size("patch")
    inv = self_term[None, :]
    chip = [(i, i ^ 1) for i in range(count)]
    links = [(i, i + 1) for i in range(1, count - 1, 2)]
    links = links + [(b, a) for a, b in links]
    beyond = [(i, i + 3) for i in range(1, count - 3, 2)]
    beyond = beyond + [(b, a) for a, b in beyond]
    product = 2 * OWN * OWN

    pairs = [
        (p * 4 + (g + p) % 4, p * 4 + ((g ^ 1) + p) % 4) for p in range(count) for g in range(4)
    ]
    half, direct = call(
        parts_body,
        (bf16(2, WAVES, PATCH), bf16(DIRECT, WAVES, PATCH)),
        [HBM],
        (HBM, HBM),
        (in_hbm(history),),
        1,
        3 * 2**20,
        [pltpu.SemaphoreType.DMA((2,))],
    )
    mine = lax.ppermute(half, "patch", links)
    cross = lax.ppermute(direct, "patch", links)
    side = lax.ppermute(history, "patch", chip)
    codes = pltpu.SMEM((SLOTS + 2 * UNROLL,), jnp.int32)

    near, inv, newest, home_codes, far_codes = call(
        lists_body,
        (pltpu.VMEM((OWN, EDGE + BLK), jnp.bfloat16), f32(1, OWN), bf16(WAVES, OWN), codes, codes),
        [SMEM] + [HBM] * 6,
        (VMEM,) * 3 + (SMEM,) * 2,
        (live_count,)
        + tuple(in_hbm(x) for x in (slot_row, slot_col, slot_delay, inv, history, near_field)),
        10**6,
        12 * 10**6,
        [
            pltpu.SMEM((SLOTS,), jnp.int32),
            pltpu.SMEM((SLOTS,), jnp.int32),
            pltpu.SMEM((SLOTS,), jnp.int32),
            pltpu.SemaphoreType.DMA((5 + OWN // ROWS,)),
        ],
    )
    near = in_vmem(near)
    mine, newest = lax.optimization_barrier((mine, newest))
    other = lax.ppermute(mine, ("patch", "grp"), pairs)
    home_codes, far_codes = (pltpu.with_memory_space_constraint(x, pltpu.SMEM) for x in (home_codes, far_codes))
    first, coupling, second, inner = call(
        response_1_body,
        (bf16(BLK, OWN), f32(WAVES, OWN), bf16(BLK, OWN), bf16(3 * BLK, BLK)),
        [VMEM] * 3,
        (VMEM,) * 4,
        (near, inv, newest),
        product * 144,
        12 * 10**6,
    )
    values, own = in_vmem(ret_values), in_vmem(history)
    both, third, corners = call(
        response_23_body,
        (bf16(2 * BLK, OWN), bf16(2 * BLK, OWN), bf16(3 * BLK, BLK)),
        [VMEM] * 5,
        (VMEM,) * 3,
        (near, inv, first, second, lax.ppermute(inner, "patch", chip)),
        product * 256,
        8 * 2**20,
    )
    acc = call(
        home_body,
        f32(RB, WAVES, BLK),
        [SMEM] + [VMEM] * 3 + [HBM],
        VMEM,
        (home_codes, values, own, in_vmem(side), third),
        2 * 10**9,
        10 * 10**6,
    )
    rhs, x, inner = call(
        second_body,
        (f32(WAVES, OWN), bf16(WAVES, OWN), bf16(WAVES, BLK)),
        [SMEM] + [VMEM] * 10 + [HBM],
        (VMEM,) * 3,
        (far_codes, values, near, in_vmem(cross), in_vmem(mine), in_vmem(other), in_vmem(side), acc, coupling, incident, inv, third),
        10**9,
        10**6,
        [pltpu.VMEM((RB, WAVES, BLK), jnp.float32)],
    )
    edge = lax.ppermute(inner, "patch", chip)
    coupling = call(own_body, f32(WAVES, OWN), [VMEM] * 2, VMEM, (x, near), product * 16, 8 * 2**20)
    y, far = call(
        side_body,
        (bf16(WAVES, OWN), bf16(2 * WAVES, OWN)),
        [VMEM] * 6,
        (VMEM,) * 2,
        (near, edge, coupling, rhs, inv, x),
        product,
        2**19,
    )
    edge = lax.ppermute(far, "patch", chip)
    far = lax.ppermute(far, "patch", beyond)
    near_by = call(
        early_body,
        bf16(3 * WAVES + 3 * BLK, BLK),
        [VMEM] * 7,
        VMEM,
        (near, x, y, edge, rhs, inv, corners),
        product,
        2**19,
    )
    near_by = lax.ppermute(near_by, "patch", links)
    y_3, inner = call(
        whole_body,
        (bf16(WAVES, OWN), bf16(WAVES, BLK)),
        [VMEM] * 5,
        (VMEM,) * 2,
        (near, y, edge, rhs, inv),
        product * 16,
        8 * 2**20,
    )
    edge = lax.ppermute(inner, "patch", chip)
    coupling = call(
        own_body, f32(WAVES, OWN), [VMEM] * 2, VMEM, (y_3, near), product * 16, 8 * 2**20
    )
    shared, mine_3 = call(
        edges_body,
        (bf16(2 * WAVES, BLK), bf16(WAVES, BLK)),
        [VMEM] * 5 + [HBM] * 2,
        (VMEM,) * 2,
        (near_by, far, first, x, y, coupling, edge),
        product // 100,
        2**17,
    )
    other = lax.ppermute(shared, "patch", chip)
    partial = call(
        own_part_body,
        f32(WAVES, OWN),
        [VMEM] * 10,
        VMEM,
        (near, edge, coupling, rhs, inv, shared, mine_3, first, both, third),
        product * 3,
        2**21,
    )
    current, x = call(
        last_body,
        (pltpu.VMEM((WAVES, OWN), jnp.float32), bf16(WAVES, OWN)),
        [VMEM] * 4,
        (VMEM,) * 2,
        (partial, other, both, third),
        product * 2,
        2**20,
    )
    turns = [
        lax.ppermute(x, "grp", [(i, i ^ k) for i in range(4)]) for k in (1, 3, 2)
    ]
    newest = call(
        join_body,
        bf16(WAVES, PATCH),
        [VMEM] * 4,
        HBM,
        (x, *turns),
        0,
        2**20,
        [pltpu.SemaphoreType.DMA((4,))],
    )
    return current, newest


def solution(mesh):
    placed = (
        P(None, ("patch", "grp")),
        P(("patch", "grp")),
        P(("patch", "grp"), None),
        P(None, None, "patch"),
        P(("patch", "grp"), None, None),
        P(("patch", "grp")),
        P(("patch", "grp")),
        P(("patch", "grp")),
        P(("patch", "grp")),
    )
    return jax.shard_map(
        body,
        mesh=mesh,
        in_specs=placed,
        out_specs=(P(None, ("patch", "grp")), P(None, "patch")),
        check_vma=False,
    )
```
